32 devices in a mesh: pipe: 2 (over y), expert: 4 (over z), tensor: 4 (over x, core).
Axes of the slice: x: 2, y: 2, z: 4, core: 2. Of those that a mesh axis runs over, the one named last changes fastest.
Arguments:
- stream: bfloat16 [1024, 6144], P(('pipe', 'expert'), 'tensor')
- norm_gain: float32 [6144], P('tensor'), may hold values from 0.5 to 1.5
- attn_gain: float32 [6144], P('tensor'), may hold values from 0.5 to 1.5
- router: float32 [6144, 4], P('tensor'), may hold values from -0.078125 to 0.078125
- expert_ids: int32 [1024, 2], P(('pipe', 'expert')), may hold values from 0 to 3, as said below
- expert_slots: int32 [1024, 2], P(('pipe', 'expert')), may hold values from -1 to 39, as said below
- w_gate: bfloat16 [4, 6144, 8192], P('expert', None, ('pipe', 'tensor')), may hold values from -0.078125 to 0.078125
- w_up: bfloat16 [4, 6144, 8192], P('expert', None, ('pipe', 'tensor')), may hold values from -0.078125 to 0.078125
- w_down: bfloat16 [4, 8192, 6144], P('expert', ('pipe', 'tensor')), may hold values from -0.09375 to 0.09375
- w_query: bfloat16 [6144, 6144], P('tensor', ('pipe', 'expert'))
- w_key: bfloat16 [6144, 1024], P('tensor')
- w_value: bfloat16 [6144, 1024], P('tensor'), may hold values from -0.078125 to 0.078125
Outputs:
- new_stream: bfloat16 [1024, 6144], P(('pipe', 'expert'), 'tensor')
- attended: bfloat16 [1024, 6144], P('tensor', ('pipe', 'expert'))
The draws below stay inside these ranges and needn't reach their ends.
Inputs may be any that keep to these rules, and one draw needn't show every extreme that they name: `expert_ids`: each row names two different experts. `expert_slots`: within the rows of one group of 128 tokens, each expert's picks take slots 0, 1, 2 and so on in token order (pick 0 before pick 1) until 40 are taken, later picks of that expert are -1; so each pair of expert and slot is named at most once in a group.
All inputs are finite; a program needn't handle non-finite values.
Results may differ from the reference program's by a relative error of at most 0.015.
Values may be sent and summed in bfloat16 or wider, within the bound.
A program may use at most 128 MiB of HBM per device.

```python
import math
import jax
import jax.numpy as jnp
from jax import lax

D = 6144
FF = 8192
QH = 48
KVH = 8
HD = 128
TOK_DEV = 128
EXPERTS = 4
TOKENS = 1024
CAP = 40
N_PIPE = 2
N_EXPERT = 4


def routing(base_key):
    key_base, key_global, key_block = jax.random.split(base_key, 3)
    groups = TOKENS // TOK_DEV
    noise = jax.random.randint(key_base, (TOKENS, EXPERTS), 0, 64)
    favour = jax.random.permutation(key_global, EXPERTS) * 4
    block_keys = jax.random.split(key_block, groups)
    local_bias = jax.vmap(lambda single: jax.random.permutation(single, EXPERTS))(block_keys) * 2
    scores = noise + favour[None, :] + jnp.repeat(local_bias, TOK_DEV, axis=0)
    distinct = scores * EXPERTS + jnp.arange(EXPERTS, dtype=jnp.int32)[None, :]
    picks = lax.top_k(distinct, 2)[1].astype(jnp.int32)
    marks = (picks[:, :, None] == jnp.arange(EXPERTS, dtype=jnp.int32)[None, None, :]).astype(jnp.int32)
    marks = marks.reshape(groups, TOK_DEV * 2, EXPERTS)
    ranks = jnp.cumsum(marks, axis=1) - marks
    slot_rank = jnp.sum(ranks * marks, axis=2).reshape(TOKENS, 2)
    slots = jnp.where(slot_rank < CAP, slot_rank, -1).astype(jnp.int32)
    return (picks, slots)


def key_matrix(base_key):
    return jax.random.normal(jax.random.fold_in(base_key, 5), (D, KVH * HD), jnp.float32) * D ** (-0.5)


def draw_expert_ids(key, part):
    picks, slots = routing(key)
    return picks


def draw_expert_slots(key, part):
    picks, slots = routing(key)
    return slots


def draw_w_key(key, part):
    shared = key_matrix(key)
    return shared.astype(jnp.bfloat16)


def draw_w_query(key, part):
    key = jax.random.fold_in(key, 43)
    key_drawn = jax.random.fold_in(key, 0)
    drawn = jax.random.normal(key_drawn, (D, QH * HD), jnp.float32) * D ** (-0.5)
    return drawn.astype(jnp.bfloat16)


def draw_stream(key, part):
    key = jax.random.fold_in(key, 11)
    key_values, key_rows = jax.random.split(key)
    column = jnp.arange(D, dtype=jnp.float32) / D
    values = jax.random.normal(key_values, (TOKENS, D), jnp.float32)
    column_scale = 10.0 ** column
    row_scale = jnp.exp(jax.random.uniform(key_rows, (TOKENS, 1), jnp.float32, 0.0, math.log(10.0)))
    return (values * column_scale[None, :] * row_scale * 0.15).astype(jnp.bfloat16)


def with_spikes(values, key, source, target, shards_of, factor):
    def block_of(position):
        return (jnp.arange(values.shape[position]) // (values.shape[position] // shards_of)).reshape((-1,) + (1,) * (values.ndim - 1 - position))

    near = jax.random.permutation(key, shards_of)[block_of(target)]
    other_side = (block_of(target) + shards_of // 2) % shards_of
    return jnp.where((block_of(source) == near) | (block_of(source) == other_side), factor * values, values)


def shard_levels(own_key, dims, cuts, least, largest):
    loudness, own = 1.0, jax.random.fold_in(own_key, 6)
    for dim, shards_of in cuts:
        heights = jnp.exp(jax.random.uniform(jax.random.fold_in(own, dim), (shards_of,), jnp.float32, least / len(cuts), largest / len(cuts)))
        loudness = loudness * jnp.repeat(heights, dims[dim] // shards_of).reshape([-1 if axis == dim else 1 for axis in range(len(dims))])
    return loudness


def normal_values(rng, shape, spread, bound, shards=(), kind=jnp.bfloat16):
    array = jax.random.normal(rng, shape, jnp.float32) * spread
    if len(shards) > 0:
        array = shard_levels(rng, shape, shards, -0.22, 0.18) * array
    return jnp.clip(array, min=-bound, max=bound).astype(kind)


def bell_draw_with(key, extent, width, most, cuts, heavy, kind=jnp.bfloat16):
    array = width * jax.random.normal(key, extent, jnp.float32)
    if cuts:
        array = array * shard_levels(key, extent, cuts, -0.22, 0.18)
    return jnp.clip(with_spikes(array, jax.random.fold_in(key, 3), *heavy), -most, most).astype(kind)


def setup_inputs(seed: int = 0) -> dict:
    arg_keys = jax.random.split(jax.random.key(seed), 13)
    stream = draw_stream(jax.random.fold_in(arg_keys[12], 71), 0)
    norm_gain = jnp.clip(1.0 + 0.1 * jax.random.normal(arg_keys[1], (D,), jnp.float32), 0.5, 1.5)
    attn_gain = jnp.clip(1.0 + 0.1 * jax.random.normal(arg_keys[2], (D,), jnp.float32), 0.5, 1.5)
    router = normal_values(arg_keys[3], (D, EXPERTS), D ** -0.5, 0.078125, ((0, 4),), jnp.float32)
    expert_ids = draw_expert_ids(jax.random.fold_in(arg_keys[12], 71), 0)
    expert_slots = draw_expert_slots(jax.random.fold_in(arg_keys[12], 71), 0)
    w_gate = normal_values(arg_keys[6], (EXPERTS, D, FF), D ** -0.5, 0.078125, ((0, 4), (2, 8)))
    w_up = normal_values(arg_keys[7], (EXPERTS, D, FF), D ** -0.5, 0.078125, ((0, 4), (2, 8)))
    w_down = bell_draw_with(arg_keys[8], (EXPERTS, FF, D), FF ** -0.5, 0.09375, ((0, 4), (1, 8)), (1, 2, 8, 2.0))
    w_query = draw_w_query(jax.random.fold_in(arg_keys[12], 71), 0)
    w_key = draw_w_key(jax.random.fold_in(arg_keys[12], 71), 0)
    w_value = normal_values(arg_keys[11], (D, KVH * HD), D ** -0.5, 0.078125, ((0, 4),))
    return {"stream": stream, "norm_gain": norm_gain, "attn_gain": attn_gain, "router": router, "expert_ids": expert_ids, "expert_slots": expert_slots, "w_gate": w_gate, "w_up": w_up, "w_down": w_down, "w_query": w_query, "w_key": w_key, "w_value": w_value}


NORM_EPS = 1e-05

def expert_apply(operands):
    buffer_rows, gate_weight, up_weight, down_weight = operands
    gate_value = jnp.dot(buffer_rows, gate_weight, preferred_element_type=jnp.float32)
    up_value = jnp.dot(buffer_rows, up_weight, preferred_element_type=jnp.float32)
    hidden_value = (jax.nn.silu(gate_value) * up_value).astype(jnp.bfloat16)
    return jnp.dot(hidden_value, down_weight, preferred_element_type=jnp.float32).astype(jnp.bfloat16)

def head_attend(operands):
    query_head, key_head, value_head = operands
    scores = jnp.dot(query_head, key_head.T, preferred_element_type=jnp.float32) * (1.0 / math.sqrt(HD))
    positions = jnp.arange(query_head.shape[0], dtype=jnp.int32)
    allowed = positions[None, :] <= positions[:, None]
    masked = jnp.where(allowed, scores, -1e+30)
    highest = lax.optimization_barrier(jnp.max(masked, axis=1, keepdims=True))
    weights = jnp.where(allowed, jnp.exp(masked - highest), 0.0)
    totals = lax.optimization_barrier(jnp.sum(weights, axis=1, keepdims=True))
    return jnp.dot(weights.astype(jnp.bfloat16), value_head, preferred_element_type=jnp.float32) / totals

def reference(stream, norm_gain, attn_gain, router, expert_ids, expert_slots, w_gate, w_up, w_down, w_query, w_key, w_value):
    groups = N_PIPE * N_EXPERT
    stream_f = stream.astype(jnp.float32)
    squares = lax.optimization_barrier(jnp.sum(stream_f * stream_f, axis=1))
    inverse = lax.rsqrt(squares / D + NORM_EPS)
    scaled = stream_f * norm_gain
    normed = (scaled * inverse[:, None]).astype(jnp.bfloat16)
    logits = inverse[:, None] * jnp.dot(scaled, router, precision=lax.Precision.HIGHEST)
    onehot = expert_ids[:, :, None] == jnp.arange(EXPERTS, dtype=jnp.int32)[None, None, :]
    picked = lax.optimization_barrier(jnp.sum(jnp.where(onehot, logits[:, None, :], 0.0), axis=2))
    first_share = jax.nn.sigmoid(picked[:, 0] - picked[:, 1])
    mixing = jnp.stack([first_share, 1.0 - first_share], axis=1)
    owner = jnp.arange(TOKENS, dtype=jnp.int32) // TOK_DEV
    slot_total = groups * EXPERTS * CAP
    target = jnp.where(expert_slots >= 0, (owner[:, None] * EXPERTS + expert_ids) * CAP + expert_slots, slot_total).astype(jnp.int32)
    copies = jnp.broadcast_to(normed[:, None, :], (TOKENS, 2, D)).reshape(TOKENS * 2, D)
    buffer = jnp.zeros((slot_total + 1, D), jnp.bfloat16).at[target.reshape(-1)].set(copies)[:slot_total]
    by_expert = buffer.reshape(groups, EXPERTS, CAP, D).transpose(1, 0, 2, 3).reshape(EXPERTS, groups * CAP, D)
    produced = lax.map(expert_apply, (by_expert, w_gate, w_up, w_down))
    returned = produced.reshape(EXPERTS, groups, CAP, D).transpose(1, 0, 2, 3).reshape(slot_total, D)
    padded = jnp.concatenate([returned, jnp.zeros((1, D), jnp.bfloat16)], axis=0)
    gathered = padded[target].astype(jnp.float32)
    moe_sum = lax.optimization_barrier(jnp.sum(mixing[:, :, None] * gathered, axis=1))
    new_stream = (stream_f + moe_sum).astype(jnp.bfloat16)
    attn_f = new_stream.astype(jnp.float32)
    inverse_two = lax.rsqrt(lax.optimization_barrier(jnp.sum(attn_f * attn_f, axis=1)) / D + NORM_EPS)
    attn_in = (attn_f * inverse_two[:, None] * attn_gain).astype(jnp.bfloat16)
    queries = jnp.dot(attn_in, w_query, preferred_element_type=jnp.float32).astype(jnp.bfloat16)
    queries = queries.reshape(TOKENS, QH, HD).transpose(1, 0, 2)
    key_rows = jnp.dot(attn_in, w_key, preferred_element_type=jnp.float32).astype(jnp.bfloat16)
    key_rows = key_rows.reshape(TOKENS, KVH, HD).transpose(1, 0, 2)
    value_rows = jnp.dot(attn_in, w_value, preferred_element_type=jnp.float32).astype(jnp.bfloat16)
    value_rows = value_rows.reshape(TOKENS, KVH, HD).transpose(1, 0, 2)
    sharing = jnp.arange(QH, dtype=jnp.int32) // (QH // KVH)
    contexts = lax.map(head_attend, (queries, key_rows[sharing], value_rows[sharing]))
    attended = contexts.transpose(1, 0, 2).reshape(TOKENS, QH * HD).astype(jnp.bfloat16)
    return (new_stream, attended)
```

```python
import functools
import math

import jax
import jax.numpy as jnp
from jax import lax
from jax.experimental import pallas as pl
from jax.experimental.pallas import tpu as pltpu
from jax.sharding import PartitionSpec as P

D = 6144
QH = 48
KVH = 8
HD = 128
CAP = 40
NORM_EPS = 1e-05
MESH = pl.DeviceIdType.MESH
MIB = 1024 * 1024


def lane_tile(width):
    return 256 if width % 256 == 0 else 128


def expert_kernel(
    np_, ne, nt, out_ref_shape, going, wg_hbm, wu_hbm, wd_hbm, back,
    rows, wg, wu, wd, lhs, acc_g, acc_u, hid, part, sib_out, sib_in, tgt_out, tgt_in, zbuf,
    w_sem, own_sem, zs, zr, cs, cr, ss, sr, bs, br, ts, tr, rs, rr,
):
    nc = nt // 2
    p = lax.axis_index("pipe")
    e = lax.axis_index("expert")
    t = lax.axis_index("tensor")
    c, k = t // 2, t % 2
    width = going.shape[2]
    hidden = wg.shape[2]
    count = np_ * ne * CAP
    sib = (p, e, c * 2 + (1 - k))

    def chip(dc, dp):
        return (lax.rem(p + dp, np_), e, lax.rem(c + dc, nc) * 2 + k)

    def plane(de):
        return (p, lax.rem(e + de, ne), t)

    chips = [(dc, dp) for dc in range(nc) for dp in range(np_) if (dc, dp) != (0, 0)]
    order = [(dc, dk) for dc in range(nc) for dk in range(2)]

    own = pltpu.make_async_copy(going.at[e], rows.at[0, 0, 0, 0], own_sem)
    own.start()
    loads = {}
    for j, (dc, dk) in enumerate(order):
        piece = lax.rem(c + dc, nc) * 2 + lax.rem(k + dk, 2)
        at = pl.ds(pl.multiple_of(piece * width, 128), width)
        loads["g", j] = pltpu.make_async_copy(wg_hbm.at[at, :], wg.at[j], w_sem.at[0, j])
        loads["u", j] = pltpu.make_async_copy(wu_hbm.at[at, :], wu.at[j], w_sem.at[1, j])
        loads["d", j] = pltpu.make_async_copy(wd_hbm.at[:, at], wd.at[j], w_sem.at[2, j])

    barrier = pltpu.get_barrier_semaphore()
    peers = [sib] + [chip(dc, dp) for dc, dp in chips] + [plane(de) for de in range(1, ne)]
    for peer in peers:
        pl.semaphore_signal(barrier, inc=1, device_id=peer, device_id_type=MESH)
    pl.semaphore_wait(barrier, len(peers))

    def send(src, dst, s_sem, r_sem, peer):
        copy = pltpu.make_async_remote_copy(
            src_ref=src, dst_ref=dst, send_sem=s_sem, recv_sem=r_sem,
            device_id=peer, device_id_type=MESH,
        )
        copy.start()
        return copy

    sent = []

    def landed(ref, s_sem, r_sem):
        pltpu.make_async_remote_copy(
            src_ref=ref, dst_ref=ref, send_sem=s_sem, recv_sem=r_sem,
            device_id=sib, device_id_type=MESH,
        ).wait_recv()

    for de in range(1, ne):
        back_de = ne - de
        sent.append(send(
            going.at[lax.rem(e + de, ne)], rows.at[0, 0, 0, back_de],
            zs.at[de], zr.at[back_de], plane(de),
        ))
    own.wait()
    for j in range(nt):
        loads["g", j].start()
        loads["u", j].start()
    for j in range(nt):
        loads["d", j].start()

    def to_sibling(dc, dp, de):
        sent.append(send(
            rows.at[dc, 0, dp, de], rows.at[dc, 1, dp, de],
            ss.at[dc, dp, de], sr.at[dc, dp, de], sib,
        ))

    zorder = [0] + [de for d in range(1, ne) for de in sorted({d, ne - d}) if d <= ne - d]
    for de in zorder:
        if de:
            landed(rows.at[0, 0, 0, de], zs.at[de], zr.at[de])
        for dc, dp in chips:
            oc, op = (nc - dc) % nc, (np_ - dp) % np_
            sent.append(send(
                rows.at[0, 0, 0, de], rows.at[oc, 0, op, de],
                cs.at[dc, dp, de], cr.at[oc, op, de], chip(dc, dp),
            ))
        to_sibling(0, 0, de)

    def arrivals(dc):
        for de in zorder:
            for dp in range(np_):
                if (dc, dp) != (0, 0):
                    landed(rows.at[dc, 0, dp, de], cs.at[dc, dp, de], cr.at[dc, dp, de])
                    to_sibling(dc, dp, de)

    lt = lane_tile(width)
    ht = lane_tile(hidden)

    def gate_up(j, dc, dk):
        if dk == 1:
            for dp in range(np_):
                for de in range(ne):
                    landed(rows.at[dc, 1, dp, de], ss.at[dc, dp, de], sr.at[dc, dp, de])

        def flat(n, carry):
            at = pl.ds(pl.multiple_of(n * lt, lt), lt)
            block = rows[dc, dk, :, :, :, at].astype(jnp.float32)
            lhs[:, at] = block.reshape(count, lt).astype(jnp.bfloat16)
            return carry

        lax.fori_loop(0, width // lt, flat, 0)
        loads["g", j].wait()
        loads["u", j].wait()

        def tile(n, carry):
            at = pl.ds(pl.multiple_of(n * ht, ht), ht)
            g = jnp.dot(lhs[...], wg[j, :, at], preferred_element_type=jnp.float32)
            u = jnp.dot(lhs[...], wu[j, :, at], preferred_element_type=jnp.float32)
            if j:
                g = g + acc_g[:, at]
                u = u + acc_u[:, at]
            if j == nt - 1:
                hid[:, at] = (g / (1.0 + jnp.exp(-g)) * u).astype(jnp.bfloat16)
            else:
                acc_g[:, at] = g
                acc_u[:, at] = u
            return carry

        lax.fori_loop(0, hidden // ht, tile, 0)

    for dc in range(nc):
        arrivals(dc)
        for dk in range(2):
            gate_up(dc * 2 + dk, dc, dk)

    for dc in reversed(range(nc)):
        j = dc * 2 + 1
        loads["d", j].wait()

        def sibling_tile(n, carry, j=j, dc=dc):
            at = pl.ds(pl.multiple_of(n * lt, lt), lt)
            y = jnp.dot(hid[...], wd[j, :, at], preferred_element_type=jnp.float32)
            sib_out[dc, :, :, :, at] = y.reshape(np_, ne, CAP, lt).astype(jnp.bfloat16)
            return carry

        lax.fori_loop(0, width // lt, sibling_tile, 0)
        sent.append(send(sib_out.at[dc], sib_in.at[dc], bs.at[dc], br.at[dc], sib))
        j = dc * 2
        loads["d", j].wait()

        def own_tile(n, carry, j=j):
            at = pl.ds(pl.multiple_of(n * lt, lt), lt)
            y = jnp.dot(hid[...], wd[j, :, at], preferred_element_type=jnp.float32)
            part[:, :, :, at] = y.reshape(np_, ne, CAP, lt)
            return carry

        lax.fori_loop(0, width // lt, own_tile, 0)
        landed(sib_in.at[dc], bs.at[dc], br.at[dc])
        for de in list(range(1, ne)) + [0]:
            for dp in range(np_):
                if (dc, dp) != (0, 0):
                    tgt_out[dc, dp, de] = (
                        part[dp, de] + sib_in[dc, dp, de].astype(jnp.float32)
                    ).astype(jnp.bfloat16)
                    oc, op = (nc - dc) % nc, (np_ - dp) % np_
                    sent.append(send(
                        tgt_out.at[dc, dp, de], tgt_in.at[oc, op, de],
                        ts.at[dc, dp, de], tr.at[oc, op, de], chip(dc, dp),
                    ))

    for de in list(range(1, ne)) + [0]:
        total = part[0, de] + sib_in[0, 0, de].astype(jnp.float32)
        for dc, dp in chips:
            landed(tgt_in.at[dc, dp, de], ts.at[dc, dp, de], tr.at[dc, dp, de])
            total = total + tgt_in[dc, dp, de].astype(jnp.float32)
        if de:
            zbuf[de] = total.astype(jnp.bfloat16)
            sent.append(send(
                zbuf.at[de], back.at[e], rs.at[de], rr.at[ne - de], plane(de),
            ))
        else:
            back[e] = total.astype(jnp.bfloat16)
    for de in range(1, ne):
        landed(back.at[lax.rem(e + de, ne)], rs.at[de], rr.at[de])
    for copy in sent:
        copy.wait_send()


def expert_layer(going, gate, up, down, sizes):
    np_, ne, nt = sizes
    nc = nt // 2
    width = going.shape[2]
    hidden = gate.shape[1]
    count = np_ * ne * CAP
    dma = pltpu.SemaphoreType.DMA
    bf, f32 = jnp.bfloat16, jnp.float32
    vm = pl.BlockSpec(memory_space=pltpu.VMEM)
    hbm = pl.BlockSpec(memory_space=pl.ANY)
    return pl.pallas_call(
        functools.partial(expert_kernel, np_, ne, nt, going.shape),
        out_shape=jax.ShapeDtypeStruct(going.shape, bf),
        in_specs=[vm, hbm, hbm, hbm],
        out_specs=vm,
        scratch_shapes=[
            pltpu.VMEM((nc, 2, np_, ne, CAP, width), bf),
            pltpu.VMEM((nt, width, hidden), bf),
            pltpu.VMEM((nt, width, hidden), bf),
            pltpu.VMEM((nt, hidden, width), bf),
            pltpu.VMEM((count, width), bf),
            pltpu.VMEM((count, hidden), f32),
            pltpu.VMEM((count, hidden), f32),
            pltpu.VMEM((count, hidden), bf),
            pltpu.VMEM((np_, ne, CAP, width), f32),
            pltpu.VMEM((nc, np_, ne, CAP, width), bf),
            pltpu.VMEM((nc, np_, ne, CAP, width), bf),
            pltpu.VMEM((nc, np_, ne, CAP, width), bf),
            pltpu.VMEM((nc, np_, ne, CAP, width), bf),
            pltpu.VMEM((ne, CAP, width), bf),
            dma((3, nt)),
            dma,
            dma((ne,)), dma((ne,)),
            dma((nc, np_, ne)), dma((nc, np_, ne)),
            dma((nc, np_, ne)), dma((nc, np_, ne)),
            dma((nc,)), dma((nc,)),
            dma((nc, np_, ne)), dma((nc, np_, ne)),
            dma((ne,)), dma((ne,)),
        ],
        compiler_params=pltpu.CompilerParams(
            collective_id=0, has_side_effects=True, vmem_limit_bytes=62 * MIB
        ),
        cost_estimate=pl.CostEstimate(
            flops=6 * count * D * hidden, bytes_accessed=6 * D * hidden, transcendentals=0
        ),
        name="expert_layer",
    )(going, gate, up, down)


def on_device(
    stream,
    norm_gain,
    attn_gain,
    router,
    expert_ids,
    expert_slots,
    w_gate,
    w_up,
    w_down,
    w_query,
    w_key,
    w_value,
):
    token_rows, local_width = stream.shape
    experts = router.shape[1]
    stream_f = stream.astype(jnp.float32)
    scaled = stream_f * norm_gain
    square_part = jnp.sum(stream_f * stream_f, axis=1)
    logit_part = jnp.dot(scaled, router, precision=lax.Precision.HIGHEST)
    squares, logit_sum = lax.psum((square_part, logit_part), "tensor")
    inverse = lax.rsqrt(squares / D + NORM_EPS)
    normed = (scaled * inverse[:, None]).astype(jnp.bfloat16)
    logits = inverse[:, None] * logit_sum
    onehot = expert_ids[:, :, None] == jnp.arange(experts, dtype=jnp.int32)[None, None, :]
    picked = jnp.sum(jnp.where(onehot, logits[:, None, :], 0.0), axis=2)
    first_share = jax.nn.sigmoid(picked[:, 0] - picked[:, 1])
    mixing = jnp.stack([first_share, 1.0 - first_share], axis=1)
    slot_total = experts * CAP
    target = jnp.where(expert_slots >= 0, expert_ids * CAP + expert_slots, slot_total)
    copies = jnp.broadcast_to(normed[:, None, :], (token_rows, 2, local_width)).reshape(
        token_rows * 2, local_width
    )
    outgoing = (
        jnp.zeros((slot_total + 1, local_width), jnp.bfloat16)
        .at[target.reshape(-1)]
        .set(copies)[:slot_total]
    )
    sizes = tuple(lax.axis_size(name) for name in ("pipe", "expert", "tensor"))
    returned = expert_layer(
        outgoing.reshape(experts, CAP, local_width), w_gate[0], w_up[0], w_down[0], sizes
    ).reshape(slot_total, local_width)
    padded = jnp.concatenate([returned, jnp.zeros((1, local_width), jnp.bfloat16)], axis=0)
    picked_rows = padded[target].astype(jnp.float32)
    moe_sum = mixing[:, 0:1] * picked_rows[:, 0] + mixing[:, 1:2] * picked_rows[:, 1]
    new_stream = (stream_f + moe_sum).astype(jnp.bfloat16)
    attn_f = new_stream.astype(jnp.float32)
    square_two = lax.psum(jnp.sum(attn_f * attn_f, axis=1), "tensor")
    attn_in = (attn_f * lax.rsqrt(square_two / D + NORM_EPS)[:, None] * attn_gain).astype(
        jnp.bfloat16
    )
    head_group = lax.axis_index(("pipe", "expert"))
    query_width = w_query.shape[1]
    heads_here = query_width // HD
    shared_head = head_group * heads_here // (QH // KVH)
    key_columns = lax.dynamic_slice_in_dim(w_key, shared_head * HD, HD, 1)
    value_columns = lax.dynamic_slice_in_dim(w_value, shared_head * HD, HD, 1)
    projector = jnp.concatenate([w_query, key_columns, value_columns], axis=1)
    partial_proj = jnp.dot(
        lax.all_gather(attn_in, ("pipe", "expert"), axis=0, tiled=True),
        projector,
        preferred_element_type=jnp.float32,
    )
    own_proj = lax.psum_scatter(partial_proj, "tensor", scatter_dimension=0, tiled=True)
    query_rows = own_proj.shape[0]
    queries = own_proj[:, :query_width].astype(jnp.bfloat16).reshape(query_rows, heads_here, HD)
    key_rows = own_proj[:, query_width : query_width + HD].astype(jnp.bfloat16)
    value_rows = own_proj[:, query_width + HD :].astype(jnp.bfloat16)
    first_row = lax.axis_index("tensor") * query_rows
    query_pos = first_row + jnp.arange(query_rows, dtype=jnp.int32)
    score_scale = 1.0 / math.sqrt(HD)
    best = jnp.full((heads_here, query_rows), -1e30, jnp.float32)
    key_piece = lax.all_gather(key_rows, "tensor", axis=0, tiled=True)
    value_piece = lax.all_gather(value_rows, "tensor", axis=0, tiled=True)
    key_pos = jnp.arange(key_piece.shape[0], dtype=jnp.int32)
    allowed = (key_pos[None, :] <= query_pos[:, None])[None, :, :]
    scores = (
        jnp.einsum("qhd,kd->hqk", queries, key_piece, preferred_element_type=jnp.float32)
        * score_scale
    )
    scores = jnp.where(allowed, scores, -1e30)
    new_best = jnp.maximum(best, jnp.max(scores, axis=2))
    weights = jnp.where(allowed, jnp.exp(scores - new_best[:, :, None]), 0.0)
    total = jnp.sum(weights, axis=2)
    update = jnp.einsum(
        "hqk,kd->hqd", weights.astype(jnp.bfloat16), value_piece, preferred_element_type=jnp.float32
    )
    accum = update
    best, total, accum = (new_best, total, accum)
    context = accum / total[:, :, None]
    attended = context.transpose(1, 0, 2).reshape(query_rows, query_width).astype(jnp.bfloat16)
    return (new_stream, attended)


def solution(mesh):
    in_specs = (
        P(("pipe", "expert"), "tensor"),
        P("tensor"),
        P("tensor"),
        P("tensor", None),
        P(("pipe", "expert"), None),
        P(("pipe", "expert"), None),
        P("expert", None, ("pipe", "tensor")),
        P("expert", None, ("pipe", "tensor")),
        P("expert", ("pipe", "tensor"), None),
        P("tensor", ("pipe", "expert")),
        P("tensor", None),
        P("tensor", None),
    )
    out_specs = (P(("pipe", "expert"), "tensor"), P("tensor", ("pipe", "expert")))
    return jax.shard_map(
        on_device, mesh=mesh, in_specs=in_specs, out_specs=out_specs, check_vma=False
    )
```

```python
import functools
import math

import jax
import jax.numpy as jnp
from jax import lax
from jax.experimental import pallas as pl
from jax.experimental.pallas import tpu as pltpu
from jax.sharding import PartitionSpec as P

D = 6144
QH = 48
KVH = 8
HD = 128
CAP = 40
NORM_EPS = 1e-05
MESH = pl.DeviceIdType.MESH
MIB = 1024 * 1024


def lane_tile(width):
    return 256 if width % 256 == 0 else 128


def expert_kernel(
    np_, ne, nt, out_ref_shape, going, wg_hbm, wu_hbm, wd_hbm, back,
    rows, wg, wu, wd, lhs, acc_g, acc_u, hid, part, sib_out, sib_in, tgt_out, tgt_in, zbuf,
    w_sem, own_sem, zs, zr, cs, cr, ss, sr, bs, br, ts, tr, rs, rr,
):
    nc = nt // 2
    p = lax.axis_index("pipe")
    e = lax.axis_index("expert")
    t = lax.axis_index("tensor")
    c, k = t // 2, t % 2
    width = going.shape[2]
    hidden = wg.shape[2]
    count = np_ * ne * CAP
    sib = (p, e, c * 2 + (1 - k))

    def chip(dc, dp):
        return (lax.rem(p + dp, np_), e, lax.rem(c + dc, nc) * 2 + k)

    def plane(de):
        return (p, lax.rem(e + de, ne), t)

    chips = [(dc, dp) for dc in range(nc) for dp in range(np_) if (dc, dp) != (0, 0)]
    order = [(dc, dk) for dc in range(nc) for dk in range(2)]

    own = pltpu.make_async_copy(going.at[e], rows.at[0, 0, 0, 0], own_sem)
    own.start()
    loads = {}
    for j, (dc, dk) in enumerate(order):
        piece = lax.rem(c + dc, nc) * 2 + lax.rem(k + dk, 2)
        at = pl.ds(pl.multiple_of(piece * width, 128), width)
        loads["g", j] = pltpu.make_async_copy(wg_hbm.at[at, :], wg.at[j], w_sem.at[0, j])
        loads["u", j] = pltpu.make_async_copy(wu_hbm.at[at, :], wu.at[j], w_sem.at[1, j])
        loads["d", j] = pltpu.make_async_copy(wd_hbm.at[:, at], wd.at[j], w_sem.at[2, j])

    barrier = pltpu.get_barrier_semaphore()
    peers = [sib] + [chip(dc, dp) for dc, dp in chips] + [plane(de) for de in range(1, ne)]
    for peer in peers:
        pl.semaphore_signal(barrier, inc=1, device_id=peer, device_id_type=MESH)
    pl.semaphore_wait(barrier, len(peers))

    def send(src, dst, s_sem, r_sem, peer):
        copy = pltpu.make_async_remote_copy(
            src_ref=src, dst_ref=dst, send_sem=s_sem, recv_sem=r_sem,
            device_id=peer, device_id_type=MESH,
        )
        copy.start()
        return copy

    sent = []

    def landed(ref, s_sem, r_sem):
        pltpu.make_async_remote_copy(
            src_ref=ref, dst_ref=ref, send_sem=s_sem, recv_sem=r_sem,
            device_id=sib, device_id_type=MESH,
        ).wait_recv()

    for de in range(1, ne):
        back_de = ne - de
        sent.append(send(
            going.at[lax.rem(e + de, ne)], rows.at[0, 0, 0, back_de],
            zs.at[de], zr.at[back_de], plane(de),
        ))
    own.wait()
    for j in range(nt):
        loads["g", j].start()
        loads["u", j].start()
    for j in range(nt):
        loads["d", j].start()

    def to_sibling(dc, dp, de):
        sent.append(send(
            rows.at[dc, 0, dp, de], rows.at[dc, 1, dp, de],
            ss.at[dc, dp, de], sr.at[dc, dp, de], sib,
        ))

    zorder = [0] + [de for d in range(1, ne) for de in sorted({d, ne - d}) if d <= ne - d]
    for de in zorder:
        if de:
            landed(rows.at[0, 0, 0, de], zs.at[de], zr.at[de])
        for dc, dp in chips:
            oc, op = (nc - dc) % nc, (np_ - dp) % np_
            sent.append(send(
                rows.at[0, 0, 0, de], rows.at[oc, 0, op, de],
                cs.at[dc, dp, de], cr.at[oc, op, de], chip(dc, dp),
            ))
        to_sibling(0, 0, de)

    def arrivals(dc):
        for de in zorder:
            for dp in range(np_):
                if (dc, dp) != (0, 0):
                    landed(rows.at[dc, 0, dp, de], cs.at[dc, dp, de], cr.at[dc, dp, de])
                    to_sibling(dc, dp, de)

    lt = lane_tile(width)
    ht = lane_tile(hidden)

    def gate_up(j, dc, dk):
        if dk == 1:
            for dp in range(np_):
                for de in range(ne):
                    landed(rows.at[dc, 1, dp, de], ss.at[dc, dp, de], sr.at[dc, dp, de])

        def flat(n, carry):
            at = pl.ds(pl.multiple_of(n * lt, lt), lt)
            block = rows[dc, dk, :, :, :, at].astype(jnp.float32)
            lhs[:, at] = block.reshape(count, lt).astype(jnp.bfloat16)
            return carry

        lax.fori_loop(0, width // lt, flat, 0)
        loads["g", j].wait()
        loads["u", j].wait()

        def tile(n, carry):
            at = pl.ds(pl.multiple_of(n * ht, ht), ht)
            g = jnp.dot(lhs[...], wg[j, :, at], preferred_element_type=jnp.float32)
            u = jnp.dot(lhs[...], wu[j, :, at], preferred_element_type=jnp.float32)
            if j:
                g = g + acc_g[:, at]
                u = u + acc_u[:, at]
            if j == nt - 1:
                hid[:, at] = (g / (1.0 + jnp.exp(-g)) * u).astype(jnp.bfloat16)
            else:
                acc_g[:, at] = g
                acc_u[:, at] = u
            return carry

        lax.fori_loop(0, hidden // ht, tile, 0)

    for dc in range(nc):
        arrivals(dc)
        for dk in range(2):
            gate_up(dc * 2 + dk, dc, dk)

    for dc in reversed(range(nc)):
        j = dc * 2 + 1
        loads["d", j].wait()

        def sibling_tile(n, carry, j=j, dc=dc):
            at = pl.ds(pl.multiple_of(n * lt, lt), lt)
            y = jnp.dot(hid[...], wd[j, :, at], preferred_element_type=jnp.float32)
            sib_out[dc, :, :, :, at] = y.reshape(np_, ne, CAP, lt).astype(jnp.bfloat16)
            return carry

        lax.fori_loop(0, width // lt, sibling_tile, 0)
        sent.append(send(sib_out.at[dc], sib_in.at[dc], bs.at[dc], br.at[dc], sib))
        j = dc * 2
        loads["d", j].wait()

        def own_tile(n, carry, j=j):
            at = pl.ds(pl.multiple_of(n * lt, lt), lt)
            y = jnp.dot(hid[...], wd[j, :, at], preferred_element_type=jnp.float32)
            part[:, :, :, at] = y.reshape(np_, ne, CAP, lt)
            return carry

        lax.fori_loop(0, width // lt, own_tile, 0)
        landed(sib_in.at[dc], bs.at[dc], br.at[dc])
        for de in list(range(1, ne)) + [0]:
            for dp in range(np_):
                if (dc, dp) != (0, 0):
                    tgt_out[dc, dp, de] = (
                        part[dp, de] + sib_in[dc, dp, de].astype(jnp.float32)
                    ).astype(jnp.bfloat16)
                    oc, op = (nc - dc) % nc, (np_ - dp) % np_
                    sent.append(send(
                        tgt_out.at[dc, dp, de], tgt_in.at[oc, op, de],
                        ts.at[dc, dp, de], tr.at[oc, op, de], chip(dc, dp),
                    ))

    for de in list(range(1, ne)) + [0]:
        total = part[0, de] + sib_in[0, 0, de].astype(jnp.float32)
        for dc, dp in chips:
            landed(tgt_in.at[dc, dp, de], ts.at[dc, dp, de], tr.at[dc, dp, de])
            total = total + tgt_in[dc, dp, de].astype(jnp.float32)
        if de:
            zbuf[de] = total.astype(jnp.bfloat16)
            sent.append(send(
                zbuf.at[de], back.at[e], rs.at[de], rr.at[ne - de], plane(de),
            ))
        else:
            back[e] = total.astype(jnp.bfloat16)
    for de in range(1, ne):
        landed(back.at[lax.rem(e + de, ne)], rs.at[de], rr.at[de])
    for copy in sent:
        copy.wait_send()


def expert_layer(going, gate, up, down, sizes):
    np_, ne, nt = sizes
    nc = nt // 2
    width = going.shape[2]
    hidden = gate.shape[1]
    count = np_ * ne * CAP
    dma = pltpu.SemaphoreType.DMA
    bf, f32 = jnp.bfloat16, jnp.float32
    vm = pl.BlockSpec(memory_space=pltpu.VMEM)
    hbm = pl.BlockSpec(memory_space=pl.ANY)
    return pl.pallas_call(
        functools.partial(expert_kernel, np_, ne, nt, going.shape),
        out_shape=jax.ShapeDtypeStruct(going.shape, bf),
        in_specs=[vm, hbm, hbm, hbm],
        out_specs=vm,
        scratch_shapes=[
            pltpu.VMEM((nc, 2, np_, ne, CAP, width), bf),
            pltpu.VMEM((nt, width, hidden), bf),
            pltpu.VMEM((nt, width, hidden), bf),
            pltpu.VMEM((nt, hidden, width), bf),
            pltpu.VMEM((count, width), bf),
            pltpu.VMEM((count, hidden), f32),
            pltpu.VMEM((count, hidden), f32),
            pltpu.VMEM((count, hidden), bf),
            pltpu.VMEM((np_, ne, CAP, width), f32),
            pltpu.VMEM((nc, np_, ne, CAP, width), bf),
            pltpu.VMEM((nc, np_, ne, CAP, width), bf),
            pltpu.VMEM((nc, np_, ne, CAP, width), bf),
            pltpu.VMEM((nc, np_, ne, CAP, width), bf),
            pltpu.VMEM((ne, CAP, width), bf),
            dma((3, nt)),
            dma,
            dma((ne,)), dma((ne,)),
            dma((nc, np_, ne)), dma((nc, np_, ne)),
            dma((nc, np_, ne)), dma((nc, np_, ne)),
            dma((nc,)), dma((nc,)),
            dma((nc, np_, ne)), dma((nc, np_, ne)),
            dma((ne,)), dma((ne,)),
        ],
        compiler_params=pltpu.CompilerParams(
            collective_id=0, has_side_effects=True, vmem_limit_bytes=62 * MIB
        ),
        cost_estimate=pl.CostEstimate(
            flops=6 * count * D * hidden, bytes_accessed=6 * D * hidden, transcendentals=0
        ),
        name="expert_layer",
    )(going, gate, up, down)


def attend_kernel(
    np_, ne, nt, x_in, gain, wq_hbm, wk_hbm, wv_hbm, out,
    xs, w, lhs, sq, mine, theirs, q, kv,
    w_sem, own_sem, zs, zr, ys, yr, ps, pr, ks, kr,
):
    p = lax.axis_index("pipe")
    e = lax.axis_index("expert")
    t = lax.axis_index("tensor")
    tb, width = x_in.shape
    qw = wq_hbm.shape[1]
    cols = w.shape[1] + HD
    groups = np_ * ne
    qr = groups * tb // nt
    per = qr // tb
    heads = qw // HD
    head = (p * ne + e) * heads // (QH // KVH)
    at_head = pl.ds(pl.multiple_of(head * HD, 128), HD)
    loads = [
        pltpu.make_async_copy(wq_hbm, w.at[:, pl.ds(0, qw)], w_sem.at[0]),
        pltpu.make_async_copy(wk_hbm.at[:, at_head], w.at[:, pl.ds(qw, HD)], w_sem.at[1]),
        pltpu.make_async_copy(wv_hbm.at[:, at_head], w.at[:, pl.ds(qw + HD, HD)], w_sem.at[2]),
    ]
    for load in loads:
        load.start()
    own = pltpu.make_async_copy(x_in, xs.at[0, e], own_sem)
    own.start()

    barrier = pltpu.get_barrier_semaphore()
    peers = [(p, lax.rem(e + de, ne), t) for de in range(1, ne)]
    peers += [(lax.rem(p + dp, np_), e, t) for dp in range(1, np_)]
    peers += [(p, e, lax.rem(t + dt, nt)) for dt in range(1, nt)]
    for peer in peers:
        pl.semaphore_signal(barrier, inc=1, device_id=peer, device_id_type=MESH)
    pl.semaphore_wait(barrier, len(peers))
    own.wait()

    def copy(src, dst, s_sem, r_sem, peer):
        return pltpu.make_async_remote_copy(
            src_ref=src, dst_ref=dst, send_sem=s_sem, recv_sem=r_sem,
            device_id=peer, device_id_type=MESH,
        )

    def shift(d, s):
        return lax.rem(e + (ne - s if d == 0 else s), ne)

    def valid(d, s):
        return e >= s if d == 0 else e + s < ne

    def onward(d, s):
        block = xs.at[0, shift(d, s - 1)]
        return copy(block, block, zs.at[d, s], zr.at[d, s], (p, shift(1 - d, 1), t))

    def may_send(d, s):
        ahead = e + 1 < ne if d == 0 else e >= 1
        return jnp.logical_and(ahead, valid(d, s - 1))

    def across(dp, d, s):
        return copy(
            xs.at[0, shift(d, s)], xs.at[np_ - dp, shift(d, s)],
            ys.at[dp, d, s], yr.at[np_ - dp, d, s], (lax.rem(p + dp, np_), e, t),
        )

    def number(dp, row):
        return lax.rem(p + dp, np_) * ne + row

    def hand_over(dp, row):
        b = number(dp, row)
        return copy(
            mine.at[dp, row], theirs.at[t, lax.rem(b, per)],
            ps.at[dp, row], pr.at[t, lax.rem(b, per)], (p, e, b // per),
        )

    lt = lane_tile(width)
    ct = lane_tile(cols - HD)

    def project(dp, row):
        sq[...] = jnp.zeros_like(sq)

        def scale(n, carry):
            at = pl.ds(pl.multiple_of(n * lt, lt), lt)
            value = xs[dp, row, :, at].astype(jnp.float32)
            scaled = value * gain[:, at]
            lhs[:, at] = jnp.clip(scaled, -1e30, 1e30).astype(jnp.bfloat16)
            square = value * value
            for i in range(lt // 128):
                sq[...] += square[:, i * 128 : (i + 1) * 128]
            return carry

        lax.fori_loop(0, width // lt, scale, 0)

        def tile(n, carry):
            at = pl.ds(pl.multiple_of(n * ct, ct), ct)
            y = jnp.dot(lhs[...], w[:, at], preferred_element_type=jnp.float32)
            mine[dp, row, :, at] = y.astype(jnp.bfloat16)
            return carry

        lax.fori_loop(0, (cols - HD) // ct, tile, 0)
        total = jnp.sum(sq[...], axis=1, keepdims=True)
        high = total.astype(jnp.bfloat16).astype(jnp.float32)
        rest = jnp.where(high < 3e38, total - high, 0.0)
        middle = rest.astype(jnp.bfloat16).astype(jnp.float32)
        lane = lax.broadcasted_iota(jnp.int32, (tb, HD), 1)
        packed = jnp.where(lane == 0, high, 0.0)
        packed = jnp.where(lane == 1, middle, packed)
        packed = jnp.where(lane == 2, rest - middle, packed)
        mine[dp, row, :, pl.ds(cols - HD, HD)] = packed.astype(jnp.bfloat16)

        @pl.when(number(dp, row) // per != t)
        def _():
            hand_over(dp, row).start()

    def start_from(d, s):
        if s + 1 < ne:
            @pl.when(may_send(d, s + 1))
            def _():
                onward(d, s + 1).start()

    def start_across(d, s):
        for dp in range(1, np_):
            across(dp, d, s).start()

    def take_across(d, s):
        for dp in range(1, np_):
            across(np_ - dp, d, s).wait_recv()
            project(dp, shift(d, s))

    start_from(0, 0)
    start_from(1, 0)
    start_across(0, 0)
    for load in loads:
        load.wait()
    project(0, shift(0, 0))
    steps = [(0, 0)]
    for s in range(1, ne):
        for d in range(2):
            @pl.when(valid(d, s))
            def _(d=d, s=s):
                arrived = xs.at[0, shift(d, s)]
                copy(arrived, arrived, zs.at[d, s], zr.at[d, s], (p, e, t)).wait_recv()
                start_from(d, s)
                start_across(d, s)
        for d in range(2):
            @pl.when(valid(d, s))
            def _(d=d, s=s):
                project(0, shift(d, s))
        if s == 1:
            take_across(0, 0)
        else:
            for d in range(2):
                @pl.when(valid(d, s - 1))
                def _(d=d, s=s):
                    take_across(d, s - 1)
    for d in range(2):
        @pl.when(valid(d, ne - 1))
        def _(d=d):
            take_across(d, ne - 1)

    for i in range(per):
        b = t * per + i
        own_dp = lax.rem(b // ne + np_ - p, np_)
        total = mine[own_dp, lax.rem(b, ne)].astype(jnp.float32)
        for dt in range(1, nt):
            other = lax.rem(t + dt, nt)
            block = theirs.at[other, i]
            copy(block, block, ps.at[0, 0], pr.at[other, i], (p, e, other)).wait_recv()
            total = total + theirs[other, i].astype(jnp.float32)
        squares = jnp.sum(total[:, cols - HD :], axis=1, keepdims=True)
        value = total[:, : cols - HD] * lax.rsqrt(squares / D + NORM_EPS)
        value = value.astype(jnp.bfloat16)
        q[i * tb : (i + 1) * tb, :] = value[:, :qw]
        kv[t, i * tb : (i + 1) * tb, :] = value[:, qw:]

    shares = [
        copy(kv.at[t], kv.at[t], ks.at[dt], kr.at[nt - dt], (p, e, lax.rem(t + dt, nt)))
        for dt in range(1, nt)
    ]
    for share in shares:
        share.start()
    for dt in range(1, nt):
        block = kv.at[lax.rem(t + dt, nt)]
        copy(block, block, ks.at[dt], kr.at[dt], (p, e, lax.rem(t + dt, nt))).wait_recv()

    tokens = nt * qr

    def one_head(h, carry):
        at = pl.ds(pl.multiple_of(h * HD, HD), HD)
        keys = kv[:, :, 0:HD].reshape(tokens, HD)
        values = kv[:, :, HD : 2 * HD].reshape(tokens, HD)
        scores = lax.dot_general(
            q[:, at], keys, (((1,), (1,)), ((), ())), preferred_element_type=jnp.float32
        ) * (1.0 / math.sqrt(HD))
        row = t * qr + lax.broadcasted_iota(jnp.int32, scores.shape, 0)
        allowed = lax.broadcasted_iota(jnp.int32, scores.shape, 1) <= row
        scores = jnp.where(allowed, scores, -1e30)
        best = jnp.max(scores, axis=1, keepdims=True)
        weights = jnp.where(allowed, jnp.exp(scores - best), 0.0)
        total = jnp.sum(weights, axis=1, keepdims=True)
        context = jnp.dot(
            weights.astype(jnp.bfloat16), values, preferred_element_type=jnp.float32
        )
        out[:, at] = (context / total).astype(jnp.bfloat16)
        return carry

    lax.fori_loop(0, heads, one_head, 0)

    for share in shares:
        share.wait_send()
    for s in range(ne):
        for d in range(2):
            if s:
                @pl.when(may_send(d, s))
                def _(d=d, s=s):
                    onward(d, s).wait_send()
            if s or d == 0:
                @pl.when(valid(d, s))
                def _(d=d, s=s):
                    for dp in range(1, np_):
                        across(dp, d, s).wait_send()
    for dp in range(np_):
        for row in range(ne):
            @pl.when(number(dp, row) // per != t)
            def _(dp=dp, row=row):
                hand_over(dp, row).wait_send()


def attention_layer(x, gain, wq, wk, wv, sizes):
    np_, ne, nt = sizes
    tb, width = x.shape
    qw = wq.shape[1]
    cols = qw + 3 * HD
    qr = np_ * ne * tb // nt
    per = qr // tb
    dma = pltpu.SemaphoreType.DMA
    bf, f32 = jnp.bfloat16, jnp.float32
    vm = pl.BlockSpec(memory_space=pltpu.VMEM)
    hbm = pl.BlockSpec(memory_space=pl.ANY)
    return pl.pallas_call(
        functools.partial(attend_kernel, np_, ne, nt),
        out_shape=jax.ShapeDtypeStruct((qr, qw), bf),
        in_specs=[vm, vm, hbm, hbm, hbm],
        out_specs=vm,
        scratch_shapes=[
            pltpu.VMEM((np_, ne, tb, width), bf),
            pltpu.VMEM((width, qw + 2 * HD), bf),
            pltpu.VMEM((tb, width), bf),
            pltpu.VMEM((tb, HD), f32),
            pltpu.VMEM((np_, ne, tb, cols), bf),
            pltpu.VMEM((nt, per, tb, cols), bf),
            pltpu.VMEM((qr, qw), bf),
            pltpu.VMEM((nt, qr, 2 * HD), bf),
            dma((3,)),
            dma,
            dma((2, ne)), dma((2, ne)),
            dma((np_, 2, ne)), dma((np_, 2, ne)),
            dma((np_, ne)), dma((nt, per)),
            dma((nt,)), dma((nt,)),
        ],
        compiler_params=pltpu.CompilerParams(
            collective_id=1, has_side_effects=True, vmem_limit_bytes=48 * MIB
        ),
        cost_estimate=pl.CostEstimate(
            flops=2 * np_ * ne * tb * width * cols,
            bytes_accessed=2 * width * cols,
            transcendentals=0,
        ),
        name="attention_layer",
    )(x, gain.reshape(1, width), wq, wk, wv)


def on_device(
    stream,
    norm_gain,
    attn_gain,
    router,
    expert_ids,
    expert_slots,
    w_gate,
    w_up,
    w_down,
    w_query,
    w_key,
    w_value,
):
    token_rows, local_width = stream.shape
    experts = router.shape[1]
    stream_f = stream.astype(jnp.float32)
    scaled = stream_f * norm_gain
    square_part = jnp.sum(stream_f * stream_f, axis=1)
    logit_part = jnp.dot(scaled, router, precision=lax.Precision.HIGHEST)
    squares, logit_sum = lax.psum((square_part, logit_part), "tensor")
    inverse = lax.rsqrt(squares / D + NORM_EPS)
    normed = (scaled * inverse[:, None]).astype(jnp.bfloat16)
    logits = inverse[:, None] * logit_sum
    onehot = expert_ids[:, :, None] == jnp.arange(experts, dtype=jnp.int32)[None, None, :]
    picked = jnp.sum(jnp.where(onehot, logits[:, None, :], 0.0), axis=2)
    first_share = jax.nn.sigmoid(picked[:, 0] - picked[:, 1])
    mixing = jnp.stack([first_share, 1.0 - first_share], axis=1)
    slot_total = experts * CAP
    target = jnp.where(expert_slots >= 0, expert_ids * CAP + expert_slots, slot_total)
    copies = jnp.broadcast_to(normed[:, None, :], (token_rows, 2, local_width)).reshape(
        token_rows * 2, local_width
    )
    outgoing = (
        jnp.zeros((slot_total + 1, local_width), jnp.bfloat16)
        .at[target.reshape(-1)]
        .set(copies)[:slot_total]
    )
    sizes = tuple(lax.axis_size(name) for name in ("pipe", "expert", "tensor"))
    returned = expert_layer(
        outgoing.reshape(experts, CAP, local_width), w_gate[0], w_up[0], w_down[0], sizes
    ).reshape(slot_total, local_width)
    padded = jnp.concatenate([returned, jnp.zeros((1, local_width), jnp.bfloat16)], axis=0)
    picked_rows = padded[target].astype(jnp.float32)
    moe_sum = mixing[:, 0:1] * picked_rows[:, 0] + mixing[:, 1:2] * picked_rows[:, 1]
    new_stream = (stream_f + moe_sum).astype(jnp.bfloat16)
    attended = attention_layer(new_stream, attn_gain, w_query, w_key, w_value, sizes)
    return (new_stream, attended)


def solution(mesh):
    in_specs = (
        P(("pipe", "expert"), "tensor"),
        P("tensor"),
        P("tensor"),
        P("tensor", None),
        P(("pipe", "expert"), None),
        P(("pipe", "expert"), None),
        P("expert", None, ("pipe", "tensor")),
        P("expert", None, ("pipe", "tensor")),
        P("expert", ("pipe", "tensor"), None),
        P("tensor", ("pipe", "expert")),
        P("tensor", None),
        P("tensor", None),
    )
    out_specs = (P(("pipe", "expert"), "tensor"), P("tensor", ("pipe", "expert")))
    return jax.shard_map(
        on_device, mesh=mesh, in_specs=in_specs, out_specs=out_specs, check_vma=False
    )
```

```python
import functools
import math

import jax
import jax.numpy as jnp
from jax import lax
from jax.experimental import pallas as pl
from jax.experimental.pallas import tpu as pltpu
from jax.sharding import PartitionSpec as P

D = 6144
QH = 48
KVH = 8
HD = 128
CAP = 40
NORM_EPS = 1e-05
MESH = pl.DeviceIdType.MESH
MIB = 1024 * 1024


def lane_tile(width):
    return 256 if width % 256 == 0 else 128


def expert_kernel(
    np_, ne, nt, out_ref_shape, going, wg_hbm, wu_hbm, wd_hbm, back,
    rows, wg, wu, wd, lhs, acc_g, acc_u, hid, part, sib_out, sib_in, tgt_out, tgt_in, zbuf,
    w_sem, own_sem, zs, zr, cs, cr, ss, sr, bs, br, ts, tr, rs, rr,
):
    nc = nt // 2
    p = lax.axis_index("pipe")
    e = lax.axis_index("expert")
    t = lax.axis_index("tensor")
    c, k = t // 2, t % 2
    width = going.shape[2]
    hidden = wg.shape[2]
    count = np_ * ne * CAP
    sib = (p, e, c * 2 + (1 - k))

    def chip(dc, dp):
        return (lax.rem(p + dp, np_), e, lax.rem(c + dc, nc) * 2 + k)

    def plane(de):
        return (p, lax.rem(e + de, ne), t)

    chips = [(dc, dp) for dc in range(nc) for dp in range(np_) if (dc, dp) != (0, 0)]
    straight = [(dc, dp) for dc, dp in chips if dc == 0 or dp == 0]
    order = [(dc, dk) for dc in range(nc) for dk in range(2)]

    own = pltpu.make_async_copy(going.at[e], rows.at[0, 0, 0, 0], own_sem)
    own.start()
    loads = {}
    for j, (dc, dk) in enumerate(order):
        piece = lax.rem(c + dc, nc) * 2 + lax.rem(k + dk, 2)
        at = pl.ds(pl.multiple_of(piece * width, 128), width)
        loads["g", j] = pltpu.make_async_copy(wg_hbm.at[at, :], wg.at[j], w_sem.at[0, j])
        loads["u", j] = pltpu.make_async_copy(wu_hbm.at[at, :], wu.at[j], w_sem.at[1, j])
        loads["d", j] = pltpu.make_async_copy(wd_hbm.at[:, at], wd.at[j], w_sem.at[2, j])

    barrier = pltpu.get_barrier_semaphore()
    peers = [sib] + [chip(dc, dp) for dc, dp in chips] + [plane(de) for de in range(1, ne)]
    for peer in peers:
        pl.semaphore_signal(barrier, inc=1, device_id=peer, device_id_type=MESH)
    pl.semaphore_wait(barrier, len(peers))

    def send(src, dst, s_sem, r_sem, peer):
        copy = pltpu.make_async_remote_copy(
            src_ref=src, dst_ref=dst, send_sem=s_sem, recv_sem=r_sem,
            device_id=peer, device_id_type=MESH,
        )
        copy.start()
        return copy

    sent = []

    def landed(ref, s_sem, r_sem):
        pltpu.make_async_remote_copy(
            src_ref=ref, dst_ref=ref, send_sem=s_sem, recv_sem=r_sem,
            device_id=sib, device_id_type=MESH,
        ).wait_recv()

    for de in range(1, ne):
        back_de = ne - de
        sent.append(send(
            going.at[lax.rem(e + de, ne)], rows.at[0, 0, 0, back_de],
            zs.at[de], zr.at[back_de], plane(de),
        ))
    own.wait()
    for j in range(nt):
        loads["g", j].start()
        loads["u", j].start()
    for j in range(nt):
        loads["d", j].start()

    def to_sibling(dc, dp, de):
        sent.append(send(
            rows.at[dc, 0, dp, de], rows.at[dc, 1, dp, de],
            ss.at[dc, dp, de], sr.at[dc, dp, de], sib,
        ))

    zorder = [0] + [de for d in range(1, ne) for de in sorted({d, ne - d}) if d <= ne - d]
    for de in zorder:
        if de:
            landed(rows.at[0, 0, 0, de], zs.at[de], zr.at[de])
        for dc, dp in straight:
            oc, op = (nc - dc) % nc, (np_ - dp) % np_
            sent.append(send(
                rows.at[0, 0, 0, de], rows.at[oc, 0, op, de],
                cs.at[dc, dp, de], cr.at[oc, op, de], chip(dc, dp),
            ))
        to_sibling(0, 0, de)

    def came(dc, dp, de):
        landed(rows.at[dc, 0, dp, de], cs.at[dc, dp, de], cr.at[dc, dp, de])
        to_sibling(dc, dp, de)

    for de in zorder:
        for dc, dp in straight:
            came(dc, dp, de)
            if dc == 0 and de % 2:
                for far in range(1, nc):
                    sent.append(send(
                        rows.at[0, 0, dp, de], rows.at[nc - far, 0, dp, de],
                        cs.at[far, dp, de], cr.at[nc - far, dp, de], chip(far, 0),
                    ))
            if dp == 0 and de % 2 == 0:
                for far in range(1, np_):
                    sent.append(send(
                        rows.at[dc, 0, 0, de], rows.at[dc, 0, np_ - far, de],
                        cs.at[dc, far, de], cr.at[dc, np_ - far, de], chip(0, far),
                    ))

    lt = lane_tile(width)
    ht = lane_tile(hidden)

    def gate_up(j, dc, dk):
        if dk == 1:
            for dp in range(np_):
                for de in range(ne):
                    landed(rows.at[dc, 1, dp, de], ss.at[dc, dp, de], sr.at[dc, dp, de])

        def flat(n, carry):
            at = pl.ds(pl.multiple_of(n * lt, lt), lt)
            block = rows[dc, dk, :, :, :, at].astype(jnp.float32)
            lhs[:, at] = block.reshape(count, lt).astype(jnp.bfloat16)
            return carry

        lax.fori_loop(0, width // lt, flat, 0)
        loads["g", j].wait()
        loads["u", j].wait()

        def tile(n, carry):
            at = pl.ds(pl.multiple_of(n * ht, ht), ht)
            g = jnp.dot(lhs[...], wg[j, :, at], preferred_element_type=jnp.float32)
            u = jnp.dot(lhs[...], wu[j, :, at], preferred_element_type=jnp.float32)
            if j:
                g = g + acc_g[:, at]
                u = u + acc_u[:, at]
            if j == nt - 1:
                hid[:, at] = (g / (1.0 + jnp.exp(-g)) * u).astype(jnp.bfloat16)
            else:
                acc_g[:, at] = g
                acc_u[:, at] = u
            return carry

        lax.fori_loop(0, hidden // ht, tile, 0)

    for dc in range(nc):
        if dc:
            for de in zorder:
                for dp in range(1, np_):
                    came(dc, dp, de)
        for dk in range(2):
            gate_up(dc * 2 + dk, dc, dk)

    zlast = list(range(1, ne)) + [0]
    for dc in reversed(range(nc)):
        j = dc * 2 + 1
        loads["d", j].wait()

        def sibling_tile(n, carry, j=j, dc=dc):
            at = pl.ds(pl.multiple_of(n * lt, lt), lt)
            y = jnp.dot(hid[...], wd[j, :, at], preferred_element_type=jnp.float32)
            sib_out[dc, :, :, :, at] = y.reshape(np_, ne, CAP, lt).astype(jnp.bfloat16)
            return carry

        lax.fori_loop(0, width // lt, sibling_tile, 0)
        sent.append(send(sib_out.at[dc], sib_in.at[dc], bs.at[dc], br.at[dc], sib))
        j = dc * 2
        loads["d", j].wait()

        def own_tile(n, carry, j=j):
            at = pl.ds(pl.multiple_of(n * lt, lt), lt)
            y = jnp.dot(hid[...], wd[j, :, at], preferred_element_type=jnp.float32)
            part[:, :, :, at] = y.reshape(np_, ne, CAP, lt)
            return carry

        lax.fori_loop(0, width // lt, own_tile, 0)
        landed(sib_in.at[dc], bs.at[dc], br.at[dc])

        def partial(dp, de, dc=dc):
            return part[dp, de] + sib_in[dc, dp, de].astype(jnp.float32)

        def ship(dc, dp, de, slot, peer):
            sent.append(send(
                tgt_out.at[dc, dp, de], tgt_in.at[slot], ts.at[dc, dp, de], tr.at[slot], peer
            ))

        def collect(dc, dp, de):
            landed(tgt_in.at[dc, dp, de], ts.at[dc, dp, de], tr.at[dc, dp, de])
            return tgt_in[dc, dp, de].astype(jnp.float32)

        if dc:
            for de in zlast:
                for dp in range(1, np_):
                    tgt_out[dc, dp, de] = partial(dp, de).astype(jnp.bfloat16)
                    if de % 2:
                        ship(dc, dp, de, (dc, np_ - dp, de), chip(0, dp))
                    else:
                        ship(dc, dp, de, (nc - dc, dp, de), chip(dc, 0))
            for de in zlast:
                tgt_out[dc, 0, de] = partial(0, de).astype(jnp.bfloat16)
                if de % 2 == 0:
                    ship(dc, 0, de, (nc - dc, 0, de), chip(dc, 0))
        else:
            for de in zlast:
                if de % 2:
                    for far in range(1, nc):
                        total = tgt_out[far, 0, de].astype(jnp.float32)
                        for dp in range(1, np_):
                            total = total + collect(far, dp, de)
                        tgt_out[far, 0, de] = total.astype(jnp.bfloat16)
                        ship(far, 0, de, (nc - far, 0, de), chip(far, 0))
                for dp in range(1, np_):
                    total = partial(dp, de)
                    if de % 2 == 0:
                        for far in range(1, nc):
                            total = total + collect(far, dp, de)
                    tgt_out[0, dp, de] = total.astype(jnp.bfloat16)
                    ship(0, dp, de, (0, np_ - dp, de), chip(0, dp))

    for de in zlast:
        total = part[0, de] + sib_in[0, 0, de].astype(jnp.float32)
        for dc, dp in straight:
            total = total + collect(dc, dp, de)
        if de:
            zbuf[de] = total.astype(jnp.bfloat16)
            sent.append(send(
                zbuf.at[de], back.at[e], rs.at[de], rr.at[ne - de], plane(de),
            ))
        else:
            back[e] = total.astype(jnp.bfloat16)
    for de in range(1, ne):
        landed(back.at[lax.rem(e + de, ne)], rs.at[de], rr.at[de])
    for copy in sent:
        copy.wait_send()


def expert_layer(going, gate, up, down, sizes):
    np_, ne, nt = sizes
    nc = nt // 2
    width = going.shape[2]
    hidden = gate.shape[1]
    count = np_ * ne * CAP
    dma = pltpu.SemaphoreType.DMA
    bf, f32 = jnp.bfloat16, jnp.float32
    vm = pl.BlockSpec(memory_space=pltpu.VMEM)
    hbm = pl.BlockSpec(memory_space=pl.ANY)
    return pl.pallas_call(
        functools.partial(expert_kernel, np_, ne, nt, going.shape),
        out_shape=jax.ShapeDtypeStruct(going.shape, bf),
        in_specs=[vm, hbm, hbm, hbm],
        out_specs=vm,
        scratch_shapes=[
            pltpu.VMEM((nc, 2, np_, ne, CAP, width), bf),
            pltpu.VMEM((nt, width, hidden), bf),
            pltpu.VMEM((nt, width, hidden), bf),
            pltpu.VMEM((nt, hidden, width), bf),
            pltpu.VMEM((count, width), bf),
            pltpu.VMEM((count, hidden), f32),
            pltpu.VMEM((count, hidden), f32),
            pltpu.VMEM((count, hidden), bf),
            pltpu.VMEM((np_, ne, CAP, width), f32),
            pltpu.VMEM((nc, np_, ne, CAP, width), bf),
            pltpu.VMEM((nc, np_, ne, CAP, width), bf),
            pltpu.VMEM((nc, np_, ne, CAP, width), bf),
            pltpu.VMEM((nc, np_, ne, CAP, width), bf),
            pltpu.VMEM((ne, CAP, width), bf),
            dma((3, nt)),
            dma,
            dma((ne,)), dma((ne,)),
            dma((nc, np_, ne)), dma((nc, np_, ne)),
            dma((nc, np_, ne)), dma((nc, np_, ne)),
            dma((nc,)), dma((nc,)),
            dma((nc, np_, ne)), dma((nc, np_, ne)),
            dma((ne,)), dma((ne,)),
        ],
        compiler_params=pltpu.CompilerParams(
            collective_id=0, has_side_effects=True, vmem_limit_bytes=62 * MIB
        ),
        cost_estimate=pl.CostEstimate(
            flops=6 * count * D * hidden, bytes_accessed=6 * D * hidden, transcendentals=0
        ),
        name="expert_layer",
    )(going, gate, up, down)


def attend_kernel(
    np_, ne, nt, x_in, gain, wq_hbm, wk_hbm, wv_hbm, out,
    xs, w, lhs, sq, mine, theirs, q, kv,
    w_sem, own_sem, zs, zr, ys, yr, ps, pr, ks, kr,
):
    p = lax.axis_index("pipe")
    e = lax.axis_index("expert")
    t = lax.axis_index("tensor")
    tb, width = x_in.shape
    qw = wq_hbm.shape[1]
    cols = w.shape[1] + HD
    groups = np_ * ne
    qr = groups * tb // nt
    per = qr // tb
    heads = qw // HD
    head = (p * ne + e) * heads // (QH // KVH)
    at_head = pl.ds(pl.multiple_of(head * HD, 128), HD)
    loads = [
        pltpu.make_async_copy(wq_hbm, w.at[:, pl.ds(0, qw)], w_sem.at[0]),
        pltpu.make_async_copy(wk_hbm.at[:, at_head], w.at[:, pl.ds(qw, HD)], w_sem.at[1]),
        pltpu.make_async_copy(wv_hbm.at[:, at_head], w.at[:, pl.ds(qw + HD, HD)], w_sem.at[2]),
    ]
    for load in loads:
        load.start()
    own = pltpu.make_async_copy(x_in, xs.at[0, e], own_sem)
    own.start()

    barrier = pltpu.get_barrier_semaphore()
    peers = [(p, lax.rem(e + de, ne), t) for de in range(1, ne)]
    peers += [(lax.rem(p + dp, np_), e, t) for dp in range(1, np_)]
    peers += [(p, e, lax.rem(t + dt, nt)) for dt in range(1, nt)]
    for peer in peers:
        pl.semaphore_signal(barrier, inc=1, device_id=peer, device_id_type=MESH)
    pl.semaphore_wait(barrier, len(peers))
    own.wait()

    def copy(src, dst, s_sem, r_sem, peer):
        return pltpu.make_async_remote_copy(
            src_ref=src, dst_ref=dst, send_sem=s_sem, recv_sem=r_sem,
            device_id=peer, device_id_type=MESH,
        )

    def shift(d, s):
        return lax.rem(e + (ne - s if d == 0 else s), ne)

    def valid(d, s):
        return e >= s if d == 0 else e + s < ne

    def onward(d, s):
        block = xs.at[0, shift(d, s - 1)]
        return copy(block, block, zs.at[d, s], zr.at[d, s], (p, shift(1 - d, 1), t))

    def may_send(d, s):
        ahead = e + 1 < ne if d == 0 else e >= 1
        return jnp.logical_and(ahead, valid(d, s - 1))

    def across(dp, d, s):
        return copy(
            xs.at[0, shift(d, s)], xs.at[np_ - dp, shift(d, s)],
            ys.at[dp, d, s], yr.at[np_ - dp, d, s], (lax.rem(p + dp, np_), e, t),
        )

    def number(dp, row):
        return lax.rem(p + dp, np_) * ne + row

    def hand_over(dp, row):
        b = number(dp, row)
        return copy(
            mine.at[dp, row], theirs.at[t, lax.rem(b, per)],
            ps.at[dp, row], pr.at[t, lax.rem(b, per)], (p, e, b // per),
        )

    lt = lane_tile(width)
    ct = lane_tile(cols - HD)

    def project(dp, row):
        sq[...] = jnp.zeros_like(sq)

        def scale(n, carry):
            at = pl.ds(pl.multiple_of(n * lt, lt), lt)
            value = xs[dp, row, :, at].astype(jnp.float32)
            scaled = value * gain[:, at]
            lhs[:, at] = jnp.clip(scaled, -1e30, 1e30).astype(jnp.bfloat16)
            square = value * value
            for i in range(lt // 128):
                sq[...] += square[:, i * 128 : (i + 1) * 128]
            return carry

        lax.fori_loop(0, width // lt, scale, 0)

        def tile(n, carry):
            at = pl.ds(pl.multiple_of(n * ct, ct), ct)
            y = jnp.dot(lhs[...], w[:, at], preferred_element_type=jnp.float32)
            mine[dp, row, :, at] = y.astype(jnp.bfloat16)
            return carry

        lax.fori_loop(0, (cols - HD) // ct, tile, 0)
        total = jnp.sum(sq[...], axis=1, keepdims=True)
        high = total.astype(jnp.bfloat16).astype(jnp.float32)
        rest = jnp.where(high < 3e38, total - high, 0.0)
        middle = rest.astype(jnp.bfloat16).astype(jnp.float32)
        lane = lax.broadcasted_iota(jnp.int32, (tb, HD), 1)
        packed = jnp.where(lane == 0, high, 0.0)
        packed = jnp.where(lane == 1, middle, packed)
        packed = jnp.where(lane == 2, rest - middle, packed)
        mine[dp, row, :, pl.ds(cols - HD, HD)] = packed.astype(jnp.bfloat16)

        @pl.when(number(dp, row) // per != t)
        def _():
            hand_over(dp, row).start()

    def start_from(d, s):
        if s + 1 < ne:
            @pl.when(may_send(d, s + 1))
            def _():
                onward(d, s + 1).start()

    def start_across(d, s):
        for dp in range(1, np_):
            across(dp, d, s).start()

    def take_across(d, s):
        for dp in range(1, np_):
            across(np_ - dp, d, s).wait_recv()
            project(dp, shift(d, s))

    start_from(0, 0)
    start_from(1, 0)
    start_across(0, 0)
    for load in loads:
        load.wait()
    project(0, shift(0, 0))
    steps = [(0, 0)]
    for s in range(1, ne):
        for d in range(2):
            @pl.when(valid(d, s))
            def _(d=d, s=s):
                arrived = xs.at[0, shift(d, s)]
                copy(arrived, arrived, zs.at[d, s], zr.at[d, s], (p, e, t)).wait_recv()
                start_from(d, s)
                start_across(d, s)
        for d in range(2):
            @pl.when(valid(d, s))
            def _(d=d, s=s):
                project(0, shift(d, s))
        if s == 1:
            take_across(0, 0)
        else:
            for d in range(2):
                @pl.when(valid(d, s - 1))
                def _(d=d, s=s):
                    take_across(d, s - 1)
    for d in range(2):
        @pl.when(valid(d, ne - 1))
        def _(d=d):
            take_across(d, ne - 1)

    for i in range(per):
        b = t * per + i
        own_dp = lax.rem(b // ne + np_ - p, np_)
        total = mine[own_dp, lax.rem(b, ne)].astype(jnp.float32)
        for dt in range(1, nt):
            other = lax.rem(t + dt, nt)
            block = theirs.at[other, i]
            copy(block, block, ps.at[0, 0], pr.at[other, i], (p, e, other)).wait_recv()
            total = total + theirs[other, i].astype(jnp.float32)
        squares = jnp.sum(total[:, cols - HD :], axis=1, keepdims=True)
        value = total[:, : cols - HD] * lax.rsqrt(squares / D + NORM_EPS)
        value = value.astype(jnp.bfloat16)
        q[i * tb : (i + 1) * tb, :] = value[:, :qw]
        kv[t, i * tb : (i + 1) * tb, :] = value[:, qw:]

    shares = [
        copy(kv.at[t], kv.at[t], ks.at[dt], kr.at[nt - dt], (p, e, lax.rem(t + dt, nt)))
        for dt in range(1, nt)
    ]
    for share in shares:
        share.start()
    for dt in range(1, nt):
        block = kv.at[lax.rem(t + dt, nt)]
        copy(block, block, ks.at[dt], kr.at[dt], (p, e, lax.rem(t + dt, nt))).wait_recv()

    tokens = nt * qr

    def one_head(h, carry):
        at = pl.ds(pl.multiple_of(h * HD, HD), HD)
        keys = kv[:, :, 0:HD].reshape(tokens, HD)
        values = kv[:, :, HD : 2 * HD].reshape(tokens, HD)
        scores = lax.dot_general(
            q[:, at], keys, (((1,), (1,)), ((), ())), preferred_element_type=jnp.float32
        ) * (1.0 / math.sqrt(HD))
        row = t * qr + lax.broadcasted_iota(jnp.int32, scores.shape, 0)
        allowed = lax.broadcasted_iota(jnp.int32, scores.shape, 1) <= row
        scores = jnp.where(allowed, scores, -1e30)
        best = jnp.max(scores, axis=1, keepdims=True)
        weights = jnp.where(allowed, jnp.exp(scores - best), 0.0)
        total = jnp.sum(weights, axis=1, keepdims=True)
        context = jnp.dot(
            weights.astype(jnp.bfloat16), values, preferred_element_type=jnp.float32
        )
        out[:, at] = (context / total).astype(jnp.bfloat16)
        return carry

    lax.fori_loop(0, heads, one_head, 0)

    for share in shares:
        share.wait_send()
    for s in range(ne):
        for d in range(2):
            if s:
                @pl.when(may_send(d, s))
                def _(d=d, s=s):
                    onward(d, s).wait_send()
            if s or d == 0:
                @pl.when(valid(d, s))
                def _(d=d, s=s):
                    for dp in range(1, np_):
                        across(dp, d, s).wait_send()
    for dp in range(np_):
        for row in range(ne):
            @pl.when(number(dp, row) // per != t)
            def _(dp=dp, row=row):
                hand_over(dp, row).wait_send()


def attention_layer(x, gain, wq, wk, wv, sizes):
    np_, ne, nt = sizes
    tb, width = x.shape
    qw = wq.shape[1]
    cols = qw + 3 * HD
    qr = np_ * ne * tb // nt
    per = qr // tb
    dma = pltpu.SemaphoreType.DMA
    bf, f32 = jnp.bfloat16, jnp.float32
    vm = pl.BlockSpec(memory_space=pltpu.VMEM)
    hbm = pl.BlockSpec(memory_space=pl.ANY)
    return pl.pallas_call(
        functools.partial(attend_kernel, np_, ne, nt),
        out_shape=jax.ShapeDtypeStruct((qr, qw), bf),
        in_specs=[vm, vm, hbm, hbm, hbm],
        out_specs=vm,
        scratch_shapes=[
            pltpu.VMEM((np_, ne, tb, width), bf),
            pltpu.VMEM((width, qw + 2 * HD), bf),
            pltpu.VMEM((tb, width), bf),
            pltpu.VMEM((tb, HD), f32),
            pltpu.VMEM((np_, ne, tb, cols), bf),
            pltpu.VMEM((nt, per, tb, cols), bf),
            pltpu.VMEM((qr, qw), bf),
            pltpu.VMEM((nt, qr, 2 * HD), bf),
            dma((3,)),
            dma,
            dma((2, ne)), dma((2, ne)),
            dma((np_, 2, ne)), dma((np_, 2, ne)),
            dma((np_, ne)), dma((nt, per)),
            dma((nt,)), dma((nt,)),
        ],
        compiler_params=pltpu.CompilerParams(
            collective_id=1, has_side_effects=True, vmem_limit_bytes=48 * MIB
        ),
        cost_estimate=pl.CostEstimate(
            flops=2 * np_ * ne * tb * width * cols,
            bytes_accessed=2 * width * cols,
            transcendentals=0,
        ),
        name="attention_layer",
    )(x, gain.reshape(1, width), wq, wk, wv)


def on_device(
    stream,
    norm_gain,
    attn_gain,
    router,
    expert_ids,
    expert_slots,
    w_gate,
    w_up,
    w_down,
    w_query,
    w_key,
    w_value,
):
    token_rows, local_width = stream.shape
    experts = router.shape[1]
    stream_f = stream.astype(jnp.float32)
    scaled = stream_f * norm_gain
    square_part = jnp.sum(stream_f * stream_f, axis=1)
    logit_part = jnp.dot(scaled, router, precision=lax.Precision.HIGHEST)
    squares, logit_sum = lax.psum((square_part, logit_part), "tensor")
    inverse = lax.rsqrt(squares / D + NORM_EPS)
    normed = (scaled * inverse[:, None]).astype(jnp.bfloat16)
    logits = inverse[:, None] * logit_sum
    onehot = expert_ids[:, :, None] == jnp.arange(experts, dtype=jnp.int32)[None, None, :]
    picked = jnp.sum(jnp.where(onehot, logits[:, None, :], 0.0), axis=2)
    first_share = jax.nn.sigmoid(picked[:, 0] - picked[:, 1])
    mixing = jnp.stack([first_share, 1.0 - first_share], axis=1)
    slot_total = experts * CAP
    target = jnp.where(expert_slots >= 0, expert_ids * CAP + expert_slots, slot_total)
    slots = jnp.arange(slot_total, dtype=jnp.int32).reshape(experts, CAP, 1)
    place = ((target[:, 0] == slots) | (target[:, 1] == slots)).astype(jnp.bfloat16)
    outgoing = jnp.einsum(
        "eci,id->ecd", place, normed, preferred_element_type=jnp.float32
    ).astype(jnp.bfloat16)
    sizes = tuple(lax.axis_size(name) for name in ("pipe", "expert", "tensor"))
    returned = expert_layer(outgoing, w_gate[0], w_up[0], w_down[0], sizes)
    columns = slots.reshape(1, experts, CAP)
    combine = jnp.where(target[:, 0, None, None] == columns, mixing[:, 0, None, None], 0.0)
    combine += jnp.where(target[:, 1, None, None] == columns, mixing[:, 1, None, None], 0.0)
    moe_sum = jnp.einsum(
        "iec,ecd->id", combine, returned.astype(jnp.float32), precision=lax.Precision.HIGHEST
    )
    new_stream = (stream_f + moe_sum).astype(jnp.bfloat16)
    attended = attention_layer(new_stream, attn_gain, w_query, w_key, w_value, sizes)
    return (new_stream, attended)


def solution(mesh):
    in_specs = (
        P(("pipe", "expert"), "tensor"),
        P("tensor"),
        P("tensor"),
        P("tensor", None),
        P(("pipe", "expert"), None),
        P(("pipe", "expert"), None),
        P("expert", None, ("pipe", "tensor")),
        P("expert", None, ("pipe", "tensor")),
        P("expert", ("pipe", "tensor"), None),
        P("tensor", ("pipe", "expert")),
        P("tensor", None),
        P("tensor", None),
    )
    out_specs = (P(("pipe", "expert"), "tensor"), P("tensor", ("pipe", "expert")))
    return jax.shard_map(
        on_device, mesh=mesh, in_specs=in_specs, out_specs=out_specs, check_vma=False
    )
```

```python
import functools
import math

import jax
import jax.numpy as jnp
from jax import lax
from jax.experimental import pallas as pl
from jax.experimental.pallas import tpu as pltpu
from jax.sharding import PartitionSpec as P

D = 6144
QH = 48
KVH = 8
HD = 128
CAP = 40
NORM_EPS = 1e-05
MESH = pl.DeviceIdType.MESH
MIB = 1024 * 1024


def lane_tile(width):
    return 256 if width % 256 == 0 else 128


def expert_kernel(
    np_, ne, nt, out_ref_shape, going, wg_hbm, wu_hbm, wd_hbm, back,
    rows, wg, wu, wd, lhs, acc_g, acc_u, hid, part, sib_out, sib_in, tgt_out, tgt_in, zbuf,
    w_sem, own_sem, zs, zr, cs, cr, ss, sr, bs, br, ts, tr, rs, rr,
):
    nc = nt // 2
    p = lax.axis_index("pipe")
    e = lax.axis_index("expert")
    t = lax.axis_index("tensor")
    c, k = t // 2, t % 2
    width = going.shape[2]
    hidden = wg.shape[2]
    count = np_ * ne * CAP
    sib = (p, e, c * 2 + (1 - k))

    def chip(dc, dp):
        return (lax.rem(p + dp, np_), e, lax.rem(c + dc, nc) * 2 + k)

    def plane(de):
        return (p, lax.rem(e + de, ne), t)

    chips = [(dc, dp) for dc in range(nc) for dp in range(np_) if (dc, dp) != (0, 0)]
    straight = [(dc, dp) for dc, dp in chips if dc == 0 or dp == 0]
    order = [(dc, dk) for dc in range(nc) for dk in range(2)]

    own = pltpu.make_async_copy(going.at[e], rows.at[0, 0, 0, 0], own_sem)
    own.start()
    loads = {}
    for j, (dc, dk) in enumerate(order):
        piece = lax.rem(c + dc, nc) * 2 + lax.rem(k + dk, 2)
        at = pl.ds(pl.multiple_of(piece * width, 128), width)
        loads["g", j] = pltpu.make_async_copy(wg_hbm.at[at, :], wg.at[j], w_sem.at[0, j])
        loads["u", j] = pltpu.make_async_copy(wu_hbm.at[at, :], wu.at[j], w_sem.at[1, j])
        loads["d", j] = pltpu.make_async_copy(wd_hbm.at[:, at], wd.at[j], w_sem.at[2, j])

    barrier = pltpu.get_barrier_semaphore()
    peers = [sib] + [chip(dc, dp) for dc, dp in chips] + [plane(de) for de in range(1, ne)]
    for peer in peers:
        pl.semaphore_signal(barrier, inc=1, device_id=peer, device_id_type=MESH)
    pl.semaphore_wait(barrier, len(peers))

    def send(src, dst, s_sem, r_sem, peer):
        copy = pltpu.make_async_remote_copy(
            src_ref=src, dst_ref=dst, send_sem=s_sem, recv_sem=r_sem,
            device_id=peer, device_id_type=MESH,
        )
        copy.start()
        return copy

    sent = []

    def landed(ref, s_sem, r_sem):
        pltpu.make_async_remote_copy(
            src_ref=ref, dst_ref=ref, send_sem=s_sem, recv_sem=r_sem,
            device_id=sib, device_id_type=MESH,
        ).wait_recv()

    for de in range(1, ne):
        back_de = ne - de
        sent.append(send(
            going.at[lax.rem(e + de, ne)], rows.at[0, 0, 0, back_de],
            zs.at[de], zr.at[back_de], plane(de),
        ))
    own.wait()
    for j in range(nt):
        loads["g", j].start()
        loads["u", j].start()
    for j in range(nt):
        loads["d", j].start()

    def to_sibling(dc, dp, de):
        sent.append(send(
            rows.at[dc, 0, dp, de], rows.at[dc, 1, dp, de],
            ss.at[dc, dp, de], sr.at[dc, dp, de], sib,
        ))

    zorder = [0] + [de for d in range(1, ne) for de in sorted({d, ne - d}) if d <= ne - d]
    for de in zorder:
        if de:
            landed(rows.at[0, 0, 0, de], zs.at[de], zr.at[de])
        for dc, dp in straight:
            oc, op = (nc - dc) % nc, (np_ - dp) % np_
            sent.append(send(
                rows.at[0, 0, 0, de], rows.at[oc, 0, op, de],
                cs.at[dc, dp, de], cr.at[oc, op, de], chip(dc, dp),
            ))
        to_sibling(0, 0, de)

    def came(dc, dp, de):
        landed(rows.at[dc, 0, dp, de], cs.at[dc, dp, de], cr.at[dc, dp, de])
        to_sibling(dc, dp, de)

    for de in zorder:
        for dc, dp in straight:
            came(dc, dp, de)
            if dc == 0 and de % 2:
                for far in range(1, nc):
                    sent.append(send(
                        rows.at[0, 0, dp, de], rows.at[nc - far, 0, dp, de],
                        cs.at[far, dp, de], cr.at[nc - far, dp, de], chip(far, 0),
                    ))
            if dp == 0 and de % 2 == 0:
                for far in range(1, np_):
                    sent.append(send(
                        rows.at[dc, 0, 0, de], rows.at[dc, 0, np_ - far, de],
                        cs.at[dc, far, de], cr.at[dc, np_ - far, de], chip(0, far),
                    ))

    lt = lane_tile(width)
    ht = lane_tile(hidden)

    def gate_up(j, dc, dk):
        if dk == 1:
            for dp in range(np_):
                for de in range(ne):
                    landed(rows.at[dc, 1, dp, de], ss.at[dc, dp, de], sr.at[dc, dp, de])

        def flat(n, carry):
            at = pl.ds(pl.multiple_of(n * lt, lt), lt)
            block = rows[dc, dk, :, :, :, at].astype(jnp.float32)
            lhs[:, at] = block.reshape(count, lt).astype(jnp.bfloat16)
            return carry

        lax.fori_loop(0, width // lt, flat, 0)
        loads["g", j].wait()
        loads["u", j].wait()

        def tile(n, carry):
            at = pl.ds(pl.multiple_of(n * ht, ht), ht)
            g = jnp.dot(lhs[...], wg[j, :, at], preferred_element_type=jnp.float32)
            u = jnp.dot(lhs[...], wu[j, :, at], preferred_element_type=jnp.float32)
            if j:
                g = g + acc_g[:, at]
                u = u + acc_u[:, at]
            if j == nt - 1:
                hid[:, at] = (g / (1.0 + jnp.exp(-g)) * u).astype(jnp.bfloat16)
            else:
                acc_g[:, at] = g
                acc_u[:, at] = u
            return carry

        lax.fori_loop(0, hidden // ht, tile, 0)

    for dc in range(nc):
        if dc:
            for de in zorder:
                for dp in range(1, np_):
                    came(dc, dp, de)
        for dk in range(2):
            gate_up(dc * 2 + dk, dc, dk)

    zlast = list(range(1, ne)) + [0]
    for dc in reversed(range(nc)):
        j = dc * 2 + 1
        loads["d", j].wait()

        def sibling_tile(n, carry, j=j, dc=dc):
            at = pl.ds(pl.multiple_of(n * lt, lt), lt)
            y = jnp.dot(hid[...], wd[j, :, at], preferred_element_type=jnp.float32)
            sib_out[dc, :, :, :, at] = y.reshape(np_, ne, CAP, lt).astype(jnp.bfloat16)
            return carry

        lax.fori_loop(0, width // lt, sibling_tile, 0)
        sent.append(send(sib_out.at[dc], sib_in.at[dc], bs.at[dc], br.at[dc], sib))
        j = dc * 2
        loads["d", j].wait()

        def own_tile(n, carry, j=j):
            at = pl.ds(pl.multiple_of(n * lt, lt), lt)
            y = jnp.dot(hid[...], wd[j, :, at], preferred_element_type=jnp.float32)
            part[:, :, :, at] = y.reshape(np_, ne, CAP, lt)
            return carry

        lax.fori_loop(0, width // lt, own_tile, 0)
        landed(sib_in.at[dc], bs.at[dc], br.at[dc])

        def partial(dp, de, dc=dc):
            return part[dp, de] + sib_in[dc, dp, de].astype(jnp.float32)

        def ship(dc, dp, de, slot, peer):
            sent.append(send(
                tgt_out.at[dc, dp, de], tgt_in.at[slot], ts.at[dc, dp, de], tr.at[slot], peer
            ))

        def collect(dc, dp, de):
            landed(tgt_in.at[dc, dp, de], ts.at[dc, dp, de], tr.at[dc, dp, de])
            return tgt_in[dc, dp, de].astype(jnp.float32)

        if dc:
            for de in zlast:
                for dp in range(1, np_):
                    tgt_out[dc, dp, de] = partial(dp, de).astype(jnp.bfloat16)
                    if de % 2:
                        ship(dc, dp, de, (dc, np_ - dp, de), chip(0, dp))
                    else:
                        ship(dc, dp, de, (nc - dc, dp, de), chip(dc, 0))
            for de in zlast:
                tgt_out[dc, 0, de] = partial(0, de).astype(jnp.bfloat16)
                if de % 2 == 0:
                    ship(dc, 0, de, (nc - dc, 0, de), chip(dc, 0))
        else:
            for de in zlast:
                if de % 2:
                    for far in range(1, nc):
                        total = tgt_out[far, 0, de].astype(jnp.float32)
                        for dp in range(1, np_):
                            total = total + collect(far, dp, de)
                        tgt_out[far, 0, de] = total.astype(jnp.bfloat16)
                        ship(far, 0, de, (nc - far, 0, de), chip(far, 0))
                for dp in range(1, np_):
                    total = partial(dp, de)
                    if de % 2 == 0:
                        for far in range(1, nc):
                            total = total + collect(far, dp, de)
                    tgt_out[0, dp, de] = total.astype(jnp.bfloat16)
                    ship(0, dp, de, (0, np_ - dp, de), chip(0, dp))

    for de in zlast:
        total = part[0, de] + sib_in[0, 0, de].astype(jnp.float32)
        for dc, dp in straight:
            total = total + collect(dc, dp, de)
        if de:
            zbuf[de] = total.astype(jnp.bfloat16)
            sent.append(send(
                zbuf.at[de], back.at[e], rs.at[de], rr.at[ne - de], plane(de),
            ))
        else:
            back[e] = total.astype(jnp.bfloat16)
    for de in range(1, ne):
        landed(back.at[lax.rem(e + de, ne)], rs.at[de], rr.at[de])
    for copy in sent:
        copy.wait_send()


def expert_layer(going, gate, up, down, sizes):
    np_, ne, nt = sizes
    nc = nt // 2
    width = going.shape[2]
    hidden = gate.shape[1]
    count = np_ * ne * CAP
    dma = pltpu.SemaphoreType.DMA
    bf, f32 = jnp.bfloat16, jnp.float32
    vm = pl.BlockSpec(memory_space=pltpu.VMEM)
    hbm = pl.BlockSpec(memory_space=pl.ANY)
    return pl.pallas_call(
        functools.partial(expert_kernel, np_, ne, nt, going.shape),
        out_shape=jax.ShapeDtypeStruct(going.shape, bf),
        in_specs=[vm, hbm, hbm, hbm],
        out_specs=vm,
        scratch_shapes=[
            pltpu.VMEM((nc, 2, np_, ne, CAP, width), bf),
            pltpu.VMEM((nt, width, hidden), bf),
            pltpu.VMEM((nt, width, hidden), bf),
            pltpu.VMEM((nt, hidden, width), bf),
            pltpu.VMEM((count, width), bf),
            pltpu.VMEM((count, hidden), f32),
            pltpu.VMEM((count, hidden), f32),
            pltpu.VMEM((count, hidden), bf),
            pltpu.VMEM((np_, ne, CAP, width), f32),
            pltpu.VMEM((nc, np_, ne, CAP, width), bf),
            pltpu.VMEM((nc, np_, ne, CAP, width), bf),
            pltpu.VMEM((nc, np_, ne, CAP, width), bf),
            pltpu.VMEM((nc, np_, ne, CAP, width), bf),
            pltpu.VMEM((ne, CAP, width), bf),
            dma((3, nt)),
            dma,
            dma((ne,)), dma((ne,)),
            dma((nc, np_, ne)), dma((nc, np_, ne)),
            dma((nc, np_, ne)), dma((nc, np_, ne)),
            dma((nc,)), dma((nc,)),
            dma((nc, np_, ne)), dma((nc, np_, ne)),
            dma((ne,)), dma((ne,)),
        ],
        compiler_params=pltpu.CompilerParams(
            collective_id=0, has_side_effects=True, vmem_limit_bytes=62 * MIB
        ),
        cost_estimate=pl.CostEstimate(
            flops=6 * count * D * hidden, bytes_accessed=6 * D * hidden, transcendentals=0
        ),
        name="expert_layer",
    )(going, gate, up, down)


def attend_kernel(
    np_, ne, nt, x_in, gain, wq_hbm, wk_hbm, wv_hbm, out,
    xs, w, lhs, sq, mine, theirs, q, kv,
    w_sem, own_sem, zs, zr, ys, yr, ps, pr, ks, kr,
):
    p = lax.axis_index("pipe")
    e = lax.axis_index("expert")
    t = lax.axis_index("tensor")
    tb, width = x_in.shape
    qw = wq_hbm.shape[1]
    cols = w.shape[1] + HD
    groups = np_ * ne
    qr = groups * tb // nt
    per = qr // tb
    heads = qw // HD
    head = (p * ne + e) * heads // (QH // KVH)
    at_head = pl.ds(pl.multiple_of(head * HD, 128), HD)
    loads = [
        pltpu.make_async_copy(wq_hbm, w.at[:, pl.ds(0, qw)], w_sem.at[0]),
        pltpu.make_async_copy(wk_hbm.at[:, at_head], w.at[:, pl.ds(qw, HD)], w_sem.at[1]),
        pltpu.make_async_copy(wv_hbm.at[:, at_head], w.at[:, pl.ds(qw + HD, HD)], w_sem.at[2]),
    ]
    for load in loads:
        load.start()
    own = pltpu.make_async_copy(x_in, xs.at[0, e], own_sem)
    own.start()

    barrier = pltpu.get_barrier_semaphore()
    peers = [(p, lax.rem(e + de, ne), t) for de in range(1, ne)]
    peers += [(lax.rem(p + dp, np_), e, t) for dp in range(1, np_)]
    peers += [(p, e, lax.rem(t + dt, nt)) for dt in range(1, nt)]
    for peer in peers:
        pl.semaphore_signal(barrier, inc=1, device_id=peer, device_id_type=MESH)
    pl.semaphore_wait(barrier, len(peers))
    own.wait()

    def copy(src, dst, s_sem, r_sem, peer):
        return pltpu.make_async_remote_copy(
            src_ref=src, dst_ref=dst, send_sem=s_sem, recv_sem=r_sem,
            device_id=peer, device_id_type=MESH,
        )

    def shift(d, s):
        return lax.rem(e + (ne - s if d == 0 else s), ne)

    def valid(d, s):
        return e >= s if d == 0 else e + s < ne

    def onward(d, s):
        block = xs.at[0, shift(d, s - 1)]
        return copy(block, block, zs.at[d, s], zr.at[d, s], (p, shift(1 - d, 1), t))

    def may_send(d, s):
        ahead = e + 1 < ne if d == 0 else e >= 1
        return jnp.logical_and(ahead, valid(d, s - 1))

    def across(dp, d, s):
        return copy(
            xs.at[0, shift(d, s)], xs.at[np_ - dp, shift(d, s)],
            ys.at[dp, d, s], yr.at[np_ - dp, d, s], (lax.rem(p + dp, np_), e, t),
        )

    def number(dp, row):
        return lax.rem(p + dp, np_) * ne + row

    def hand_over(dp, row):
        b = number(dp, row)
        return copy(
            mine.at[dp, row], theirs.at[t, lax.rem(b, per)],
            ps.at[dp, row], pr.at[t, lax.rem(b, per)], (p, e, b // per),
        )

    lt = lane_tile(width)
    ct = lane_tile(cols - HD)

    def project(dp, row):
        sq[...] = jnp.zeros_like(sq)

        def scale(n, carry):
            at = pl.ds(pl.multiple_of(n * lt, lt), lt)
            value = xs[dp, row, :, at].astype(jnp.float32)
            scaled = value * gain[:, at]
            lhs[:, at] = jnp.clip(scaled, -1e30, 1e30).astype(jnp.bfloat16)
            square = value * value
            for i in range(lt // 128):
                sq[...] += square[:, i * 128 : (i + 1) * 128]
            return carry

        lax.fori_loop(0, width // lt, scale, 0)

        def tile(n, carry):
            at = pl.ds(pl.multiple_of(n * ct, ct), ct)
            y = jnp.dot(lhs[...], w[:, at], preferred_element_type=jnp.float32)
            mine[dp, row, :, at] = y.astype(jnp.bfloat16)
            return carry

        lax.fori_loop(0, (cols - HD) // ct, tile, 0)
        total = jnp.sum(sq[...], axis=1, keepdims=True)
        high = total.astype(jnp.bfloat16).astype(jnp.float32)
        rest = jnp.where(high < 3e38, total - high, 0.0)
        middle = rest.astype(jnp.bfloat16).astype(jnp.float32)
        lane = lax.broadcasted_iota(jnp.int32, (tb, HD), 1)
        packed = jnp.where(lane == 0, high, 0.0)
        packed = jnp.where(lane == 1, middle, packed)
        packed = jnp.where(lane == 2, rest - middle, packed)
        mine[dp, row, :, pl.ds(cols - HD, HD)] = packed.astype(jnp.bfloat16)

        @pl.when(number(dp, row) // per != t)
        def _():
            hand_over(dp, row).start()

    def start_from(d, s):
        if s + 1 < ne:
            @pl.when(may_send(d, s + 1))
            def _():
                onward(d, s + 1).start()

    def start_across(d, s):
        for dp in range(1, np_):
            across(dp, d, s).start()

    def take_across(d, s):
        for dp in range(1, np_):
            across(np_ - dp, d, s).wait_recv()
            project(dp, shift(d, s))

    start_from(0, 0)
    start_from(1, 0)
    start_across(0, 0)
    for load in loads:
        load.wait()
    project(0, shift(0, 0))
    steps = [(0, 0)]
    for s in range(1, ne):
        for d in range(2):
            @pl.when(valid(d, s))
            def _(d=d, s=s):
                arrived = xs.at[0, shift(d, s)]
                copy(arrived, arrived, zs.at[d, s], zr.at[d, s], (p, e, t)).wait_recv()
                start_from(d, s)
                start_across(d, s)
        for d in range(2):
            @pl.when(valid(d, s))
            def _(d=d, s=s):
                project(0, shift(d, s))
        if s == 1:
            take_across(0, 0)
        else:
            for d in range(2):
                @pl.when(valid(d, s - 1))
                def _(d=d, s=s):
                    take_across(d, s - 1)
    for d in range(2):
        @pl.when(valid(d, ne - 1))
        def _(d=d):
            take_across(d, ne - 1)

    for i in range(per):
        b = t * per + i
        own_dp = lax.rem(b // ne + np_ - p, np_)
        total = mine[own_dp, lax.rem(b, ne)].astype(jnp.float32)
        for dt in range(1, nt):
            other = lax.rem(t + dt, nt)
            block = theirs.at[other, i]
            copy(block, block, ps.at[0, 0], pr.at[other, i], (p, e, other)).wait_recv()
            total = total + theirs[other, i].astype(jnp.float32)
        squares = jnp.sum(total[:, cols - HD :], axis=1, keepdims=True)
        value = total[:, : cols - HD] * lax.rsqrt(squares / D + NORM_EPS)
        value = value.astype(jnp.bfloat16)
        q[i * tb : (i + 1) * tb, :] = value[:, :qw]
        kv[t, i * tb : (i + 1) * tb, :] = value[:, qw:]

    nc, c, k = nt // 2, t // 2, t % 2
    sib = (p, e, c * 2 + (1 - k))

    def share(block, s_at, r_at, peer):
        return copy(kv.at[block], kv.at[block], ks.at[s_at], kr.at[r_at], peer)

    shares = [
        share(t, 2 * far, 2 * (nc - far), (p, e, lax.rem(c + far, nc) * 2 + k))
        for far in range(1, nc)
    ]
    shares.append(share(t, 1, 1, sib))
    for one in shares:
        one.start()
    for far in range(1, nc):
        block = lax.rem(c + far, nc) * 2 + k
        share(block, 2 * far, 2 * far, sib).wait_recv()
        relay = share(block, 2 * far + 1, 2 * far + 1, sib)
        relay.start()
        shares.append(relay)
    for far in range(nc):
        block = lax.rem(c + far, nc) * 2 + (1 - k)
        share(block, 2 * far + 1, 2 * far + 1, sib).wait_recv()

    tokens = nt * qr

    def one_head(h, carry):
        at = pl.ds(pl.multiple_of(h * HD, HD), HD)
        keys = kv[:, :, 0:HD].reshape(tokens, HD)
        values = kv[:, :, HD : 2 * HD].reshape(tokens, HD)
        scores = lax.dot_general(
            q[:, at], keys, (((1,), (1,)), ((), ())), preferred_element_type=jnp.float32
        ) * (1.0 / math.sqrt(HD))
        row = t * qr + lax.broadcasted_iota(jnp.int32, scores.shape, 0)
        allowed = lax.broadcasted_iota(jnp.int32, scores.shape, 1) <= row
        scores = jnp.where(allowed, scores, -1e30)
        best = jnp.max(scores, axis=1, keepdims=True)
        weights = jnp.where(allowed, jnp.exp(scores - best), 0.0)
        total = jnp.sum(weights, axis=1, keepdims=True)
        context = jnp.dot(
            weights.astype(jnp.bfloat16), values, preferred_element_type=jnp.float32
        )
        out[:, at] = (context / total).astype(jnp.bfloat16)
        return carry

    lax.fori_loop(0, heads, one_head, 0)

    for one in shares:
        one.wait_send()
    for s in range(ne):
        for d in range(2):
            if s:
                @pl.when(may_send(d, s))
                def _(d=d, s=s):
                    onward(d, s).wait_send()
            if s or d == 0:
                @pl.when(valid(d, s))
                def _(d=d, s=s):
                    for dp in range(1, np_):
                        across(dp, d, s).wait_send()
    for dp in range(np_):
        for row in range(ne):
            @pl.when(number(dp, row) // per != t)
            def _(dp=dp, row=row):
                hand_over(dp, row).wait_send()


def attention_layer(x, gain, wq, wk, wv, sizes):
    np_, ne, nt = sizes
    tb, width = x.shape
    qw = wq.shape[1]
    cols = qw + 3 * HD
    qr = np_ * ne * tb // nt
    per = qr // tb
    dma = pltpu.SemaphoreType.DMA
    bf, f32 = jnp.bfloat16, jnp.float32
    vm = pl.BlockSpec(memory_space=pltpu.VMEM)
    hbm = pl.BlockSpec(memory_space=pl.ANY)
    return pl.pallas_call(
        functools.partial(attend_kernel, np_, ne, nt),
        out_shape=jax.ShapeDtypeStruct((qr, qw), bf),
        in_specs=[vm, vm, hbm, hbm, hbm],
        out_specs=vm,
        scratch_shapes=[
            pltpu.VMEM((np_, ne, tb, width), bf),
            pltpu.VMEM((width, qw + 2 * HD), bf),
            pltpu.VMEM((tb, width), bf),
            pltpu.VMEM((tb, HD), f32),
            pltpu.VMEM((np_, ne, tb, cols), bf),
            pltpu.VMEM((nt, per, tb, cols), bf),
            pltpu.VMEM((qr, qw), bf),
            pltpu.VMEM((nt, qr, 2 * HD), bf),
            dma((3,)),
            dma,
            dma((2, ne)), dma((2, ne)),
            dma((np_, 2, ne)), dma((np_, 2, ne)),
            dma((np_, ne)), dma((nt, per)),
            dma((nt,)), dma((nt,)),
        ],
        compiler_params=pltpu.CompilerParams(
            collective_id=1, has_side_effects=True, vmem_limit_bytes=48 * MIB
        ),
        cost_estimate=pl.CostEstimate(
            flops=2 * np_ * ne * tb * width * cols,
            bytes_accessed=2 * width * cols,
            transcendentals=0,
        ),
        name="attention_layer",
    )(x, gain.reshape(1, width), wq, wk, wv)


def on_device(
    stream,
    norm_gain,
    attn_gain,
    router,
    expert_ids,
    expert_slots,
    w_gate,
    w_up,
    w_down,
    w_query,
    w_key,
    w_value,
):
    token_rows, local_width = stream.shape
    experts = router.shape[1]
    stream_f = stream.astype(jnp.float32)
    scaled = stream_f * norm_gain
    square_part = jnp.sum(stream_f * stream_f, axis=1)
    logit_part = jnp.dot(scaled, router, precision=lax.Precision.HIGHEST)
    squares, logit_sum = lax.psum((square_part, logit_part), "tensor")
    inverse = lax.rsqrt(squares / D + NORM_EPS)
    normed = (scaled * inverse[:, None]).astype(jnp.bfloat16)
    logits = inverse[:, None] * logit_sum
    onehot = expert_ids[:, :, None] == jnp.arange(experts, dtype=jnp.int32)[None, None, :]
    picked = jnp.sum(jnp.where(onehot, logits[:, None, :], 0.0), axis=2)
    first_share = jax.nn.sigmoid(picked[:, 0] - picked[:, 1])
    mixing = jnp.stack([first_share, 1.0 - first_share], axis=1)
    slot_total = experts * CAP
    target = jnp.where(expert_slots >= 0, expert_ids * CAP + expert_slots, slot_total)
    slots = jnp.arange(slot_total, dtype=jnp.int32).reshape(experts, CAP, 1)
    place = ((target[:, 0] == slots) | (target[:, 1] == slots)).astype(jnp.bfloat16)
    outgoing = jnp.einsum(
        "eci,id->ecd", place, normed, preferred_element_type=jnp.float32
    ).astype(jnp.bfloat16)
    sizes = tuple(lax.axis_size(name) for name in ("pipe", "expert", "tensor"))
    returned = expert_layer(outgoing, w_gate[0], w_up[0], w_down[0], sizes)
    columns = slots.reshape(1, experts, CAP)
    combine = jnp.where(target[:, 0, None, None] == columns, mixing[:, 0, None, None], 0.0)
    combine += jnp.where(target[:, 1, None, None] == columns, mixing[:, 1, None, None], 0.0)
    moe_sum = jnp.einsum(
        "iec,ecd->id", combine, returned.astype(jnp.float32), precision=lax.Precision.HIGHEST
    )
    new_stream = (stream_f + moe_sum).astype(jnp.bfloat16)
    attended = attention_layer(new_stream, attn_gain, w_query, w_key, w_value, sizes)
    return (new_stream, attended)


def solution(mesh):
    in_specs = (
        P(("pipe", "expert"), "tensor"),
        P("tensor"),
        P("tensor"),
        P("tensor", None),
        P(("pipe", "expert"), None),
        P(("pipe", "expert"), None),
        P("expert", None, ("pipe", "tensor")),
        P("expert", None, ("pipe", "tensor")),
        P("expert", ("pipe", "tensor"), None),
        P("tensor", ("pipe", "expert")),
        P("tensor", None),
        P("tensor", None),
    )
    out_specs = (P(("pipe", "expert"), "tensor"), P("tensor", ("pipe", "expert")))
    return jax.shard_map(
        on_device, mesh=mesh, in_specs=in_specs, out_specs=out_specs, check_vma=False
    )
```
